256 devices in a mesh: seq: 256 (over y, z, x, core).
Axes of the slice: x: 4, y: 4, z: 8, core: 2. Of those that a mesh axis runs over, the one named last changes fastest.
Arguments:
- inputs: bfloat16 [131072, 3072], P('seq'), may hold values from -6 to 6
- query_proj: bfloat16 [131072, 192], P('seq'), may hold values from -6 to 6
- key_proj: bfloat16 [131072, 192], P('seq'), may hold values from -6 to 6
- value_proj: bfloat16 [131072, 192], P('seq'), may hold values from -6 to 6
- grad_out: bfloat16 [131072, 192], P('seq'), may hold values from -6 to 6
Outputs:
- query_weight_grad: float32 [3072, 192], P('seq')
- key_weight_grad: float32 [3072, 192], P('seq')
- value_weight_grad: float32 [3072, 192], P('seq')
The draws below stay inside these ranges and needn't reach their ends.
All inputs are finite; a program needn't handle non-finite values.
Results may differ from the reference program's by a relative error of at most 0.0041.
Values sent between devices are 32-bit elements; how exact they have to be, the bound alone decides.
No kernel may reach another device: no remote copies, remote signals or barrier semaphores. Data moves between devices by JAX's collectives and lax.ppermute only.
A program may use at most 192 MiB of HBM per device.

```python
import math
import jax
import jax.numpy as jnp
from jax import lax

D = 3072
HEAD = 96
HEADS = 2
TOK_DEV = 512
TOKENS = 131072


def shard_levels(key, extent, split, least, top_value):
    def one(dim, parts):
        heights = jax.random.uniform(jax.random.fold_in(jax.random.fold_in(key, 6), dim), (parts,), jnp.float32, least / len(split), top_value / len(split))
        return jnp.repeat(jnp.exp(heights), extent[dim] // parts).reshape((-1,) + (1,) * (len(extent) - dim - 1))

    gain = one(*split[0])
    for cut in split[1:]:
        gain = gain * one(*cut)
    return gain


def scatter_about(own_key, extent, scale, bound, shards=(), dtype=jnp.bfloat16):
    array = scale * jax.random.normal(own_key, extent, jnp.float32)
    if shards:
        array = array * shard_levels(own_key, extent, shards, -0.22, 0.18)
    return jnp.clip(array, -bound, bound).astype(dtype)


def setup_inputs(seed: int = 0) -> dict:
    key_list = jax.random.split(jax.random.key(seed), 6)
    inputs = scatter_about(key_list[0], (TOKENS, D), 1.0, 6.0, ((0, 256),))
    query_proj = scatter_about(key_list[1], (TOKENS, HEADS * HEAD), 1.0, 6.0, ((0, 256),))
    key_proj = scatter_about(key_list[2], (TOKENS, HEADS * HEAD), 1.0, 6.0, ((0, 256),))
    value_proj = scatter_about(key_list[3], (TOKENS, HEADS * HEAD), 1.0, 6.0, ((0, 256),))
    grad_out = scatter_about(key_list[4], (TOKENS, HEADS * HEAD), 1.0, 6.0, ((0, 256),))
    return {"inputs": inputs, "query_proj": query_proj, "key_proj": key_proj, "value_proj": value_proj, "grad_out": grad_out}


def widen(array_in):
    return array_in.astype(jnp.float32)

def round_state(state):
    narrow = lax.optimization_barrier(state.astype(jnp.bfloat16))
    return widen(narrow)

def block_grads(block_in):
    queries, keys_in, values_in, grad_rows, before, later_sum = block_in
    length = queries.shape[0]
    factor = 1.0 / (math.sqrt(HEAD) * TOKENS)
    position = jnp.arange(length)
    causal = (position[:, None] <= position[None, :])[None]
    query_wide = widen(queries)
    key_wide = widen(keys_in)
    value_wide = widen(values_in)
    grad_wide = widen(grad_rows)
    value_grad = jnp.einsum('sha,tha->hst', value_wide, grad_wide)
    value_grad = widen(jnp.where(causal, value_grad, 0.0).astype(jnp.bfloat16))
    key_query = jnp.einsum('sha,tha->hst', key_wide, query_wide)
    key_query = widen(jnp.where(causal, key_query, 0.0).astype(jnp.bfloat16))
    before_b = round_state(before)
    later_b = round_state(later_sum)
    query_grad = jnp.einsum('hst,sha->tha', value_grad, key_wide) + jnp.einsum('thb,hab->tha', grad_wide, before_b)
    key_grad = jnp.einsum('hst,tha->sha', value_grad, query_wide) + jnp.einsum('shb,hab->sha', value_wide, later_b)
    val_grad = jnp.einsum('hst,thb->shb', key_query, grad_wide) + jnp.einsum('sha,hab->shb', key_wide, later_b)
    width = HEADS * HEAD
    return ((factor * query_grad).astype(jnp.bfloat16).reshape(length, width), (factor * key_grad).astype(jnp.bfloat16).reshape(length, width), (factor * val_grad).astype(jnp.bfloat16).reshape(length, width))

def reference(inputs, query_proj, key_proj, value_proj, grad_out):
    blocks = TOKENS // TOK_DEV
    shape = (blocks, TOK_DEV, HEADS, HEAD)
    queries = query_proj.reshape(shape)
    keys_in = key_proj.reshape(shape)
    values_in = value_proj.reshape(shape)
    grad_rows = grad_out.reshape(shape)
    key_state = jnp.einsum('ctha,cthb->chab', widen(keys_in), widen(values_in))
    query_state = jnp.einsum('ctha,cthb->chab', widen(queries), widen(grad_rows))
    empty = jnp.zeros((1, HEADS, HEAD, HEAD), jnp.float32)
    before = jnp.concatenate([empty, jnp.cumsum(key_state, axis=0)[:-1]], axis=0)
    reverse_sum = jnp.flip(jnp.cumsum(jnp.flip(query_state, 0), axis=0), 0)
    later_sum = jnp.concatenate([reverse_sum[1:], empty], axis=0)
    query_grad, key_grad, val_grad = lax.map(block_grads, (queries, keys_in, values_in, grad_rows, before, later_sum))
    width = HEADS * HEAD
    stacked = jnp.concatenate([query_grad.reshape(TOKENS, width), key_grad.reshape(TOKENS, width), val_grad.reshape(TOKENS, width)], axis=1)
    summed = lax.dot_general(inputs, stacked, (((0,), (0,)), ((), ())), preferred_element_type=jnp.float32)
    return (summed[:, :width], summed[:, width:2 * width], summed[:, 2 * width:])
```

```python
import functools
import math

import jax
import jax.numpy as jnp
from jax import lax
from jax.experimental import pallas as pl
from jax.experimental.pallas import tpu as pltpu
from jax.sharding import PartitionSpec as P

HEAD = 96
NY, NZ, NX, NC = 4, 8, 4, 2
SEQ = "seq"
F32 = jnp.float32
BF16 = jnp.bfloat16


def coords(i):
    c, i = i % NC, i // NC
    x, i = i % NX, i // NX
    return i // NZ, i % NZ, x, c


def index(y, z, x, c):
    return ((y * NZ + z) * NX + x) * NC + c


def permute(value, move):
    count = NY * NZ * NX * NC
    return lax.ppermute(value, SEQ, [(i, index(*move(*coords(i)))) for i in range(count)])


def swap_cores(value):
    return permute(value, lambda y, z, x, c: (y, z, x, 1 - c))


def along_x(d):
    return lambda y, z, x, c: (y, z, (x + d * (1 - 2 * c)) % NX, c)


def along_y(d):
    return lambda y, z, x, c: ((y + d * (1 - 2 * c)) % NY, z, x, c)


def along_z_low(d):
    return lambda y, z, x, c: (y, z // 4 * 4 + (z % 4 + d * (1 - 2 * c)) % 4, x, c)


def along_z_high(d):
    return lambda y, z, x, c: (y, (z + 4 * d) % NZ, x, c)


def first_axis(d):
    return lambda y, z, x, c: (y, z, (x + d) % NX, c) if c == 0 else ((y + d) % NY, z, x, c)


def second_axis(d):
    return lambda y, z, x, c: ((y + d) % NY, z, x, c) if c == 0 else (y, z, (x + d) % NX, c)


def z_axis(d):
    return lambda y, z, x, c: (y, (z + d) % NZ, x, c)


def rows_dot(a, b):
    return lax.dot_general(a, b, (((0,), (0,)), ((), ())), preferred_element_type=F32)


def lanes_dot(a, b):
    return lax.dot_general(a, b, (((1,), (1,)), ((), ())), preferred_element_type=F32)


def head(ref, h):
    return ref[:, h * HEAD : (h + 1) * HEAD]


def states_kernel(core, q, k, v, g, keep, send):
    first = core[0] == 0
    for h in range(2):
        rows = slice(h * HEAD, (h + 1) * HEAD)
        key_state = rows_dot(head(k, h), head(v, h))
        query_state = rows_dot(head(q, h), head(g, h))
        keep[rows, :] = jnp.where(first, key_state, query_state)
        send[rows, :] = jnp.where(first, query_state, key_state)


def local_kernel(q, k, v, g, out):
    length = q.shape[0]
    s = lax.broadcasted_iota(jnp.int32, (length, length), 0)
    t = lax.broadcasted_iota(jnp.int32, (length, length), 1)
    causal = s <= t
    width = 2 * HEAD
    for h in range(2):
        qh, kh, vh, gh = head(q, h), head(k, h), head(v, h), head(g, h)
        vg = jnp.where(causal, lanes_dot(vh, gh), 0.0).astype(BF16)
        kq = jnp.where(causal, lanes_dot(kh, qh), 0.0).astype(BF16)
        at = h * HEAD
        out[:, at : at + HEAD] = rows_dot(vg, kh)
        out[:, width + at : width + at + HEAD] = jnp.dot(vg, qh, preferred_element_type=F32)
        out[:, 2 * width + at : 2 * width + at + HEAD] = jnp.dot(kq, gh, preferred_element_type=F32)


def weight_kernel(factor, core, x, loc, k, v, g, own, other, keep, send, d, block):
    y = pl.program_id(0)
    c = core[0]

    @pl.when(y == 0)
    def _():
        width = 2 * HEAD
        first = c == 0
        before = jnp.where(first, own[...], other[...]).astype(BF16)
        later = jnp.where(first, other[...], own[...]).astype(BF16)
        for h in range(2):
            rows = slice(h * HEAD, (h + 1) * HEAD)
            parts = (
                lanes_dot(head(g, h), before[rows, :]),
                lanes_dot(head(v, h), later[rows, :]),
                jnp.dot(head(k, h), later[rows, :], preferred_element_type=F32),
            )
            for n, part in enumerate(parts):
                at = n * width + h * HEAD
                d[:, at : at + HEAD] = (factor * (loc[:, at : at + HEAD] + part)).astype(BF16)

    block[...] = rows_dot(x[...], d[...])
    for half in range(2):
        ref_for = {0: keep, 1: send}
        for role in range(2):
            ref = ref_for[role]

            @pl.when(c == (half if role == 0 else 1 - half))
            def _(ref=ref, half=half):
                for xi in range(NX):
                    for z in range(NZ):
                        at = ((z * NX + xi) * NC + half) * 12
                        value = block[at : at + 12, :]
                        if half == 0:
                            ref[xi, y, z * 12 : z * 12 + 12, :] = value
                        else:
                            ref[y, xi, z * 12 : z * 12 + 12, :] = value


VMEM = pl.BlockSpec(memory_space=pltpu.VMEM)
SMEM = pl.BlockSpec(memory_space=pltpu.SMEM)


def cost(flops, moved):
    return pl.CostEstimate(flops=flops, bytes_accessed=moved, transcendentals=0)


def states(core, q, k, v, g):
    shape = jax.ShapeDtypeStruct((2 * HEAD, HEAD), F32)
    return pl.pallas_call(
        states_kernel,
        out_shape=(shape, shape),
        in_specs=[SMEM] + [VMEM] * 4,
        out_specs=(VMEM, VMEM),
        cost_estimate=cost(4 * 512 * 192 * 192, 10**6),
    )(core, q, k, v, g)


def local(q, k, v, g):
    return pl.pallas_call(
        local_kernel,
        out_shape=jax.ShapeDtypeStruct((q.shape[0], 6 * HEAD), F32),
        in_specs=[VMEM] * 4,
        out_specs=VMEM,
        cost_estimate=cost(20 * 512 * 512 * 96, 2 * 10**6),
        compiler_params=pltpu.CompilerParams(vmem_limit_bytes=24 * 2**20),
    )(q, k, v, g)


def weight_terms(core, x, loc, k, v, g, own, other, factor):
    length, features = x.shape
    rows = features // NY
    whole = lambda a: pl.BlockSpec(a.shape, lambda y: (0,) * a.ndim)
    shape = jax.ShapeDtypeStruct((NX, NY, NZ * 12, 6 * HEAD), F32)
    out = pl.BlockSpec(shape.shape, lambda y: (0, 0, 0, 0))
    return pl.pallas_call(
        functools.partial(weight_kernel, factor),
        grid=(NY,),
        out_shape=(shape, shape),
        in_specs=[SMEM, pl.BlockSpec((length, rows), lambda y: (0, y))]
        + [whole(a) for a in (loc, k, v, g, own, other)],
        out_specs=(out, out),
        scratch_shapes=[pltpu.VMEM((length, 6 * HEAD), BF16), pltpu.VMEM((rows, 6 * HEAD), F32)],
        cost_estimate=cost(2 * 512 * 3072 * 576, 12 * 10**6),
        compiler_params=pltpu.CompilerParams(vmem_limit_bytes=48 * 2**20),
    )(core, x, loc, k, v, g, own, other)


def gather_before(total, move, count, rank):
    before = jnp.zeros_like(total)
    whole = total
    for d in range(1, count):
        came = permute(total, move(d))
        before = before + jnp.where(rank >= d, came, 0.0)
        whole = whole + came
    return before, whole


def entering(core, me, keep, send):
    y, z, x, c = me
    chip = keep + swap_cores(send)
    flip = lambda p, n: jnp.where(c == 0, p, n - 1 - p)
    before, total = gather_before(chip, along_x, NX, flip(x, NX))
    more, total = gather_before(total, along_z_low, 4, flip(z % 4, 4))
    before = before + more
    more, total = gather_before(total, along_z_high, 2, flip(z // 4, 2))
    before = before + more
    more, _ = gather_before(total, along_y, NY, flip(y, NY))
    before = before + more
    return before, swap_cores(before + keep)


def pick(array, i):
    return lax.dynamic_index_in_dim(array, i, 0, keepdims=False)


def scatter_sum(me, keep, send):
    y, z, x, c = me
    mine = jnp.where(c == 0, x, y)
    partner = jnp.where(c == 0, y, x)
    far = (2, 1, 3, 0)
    total = None
    for d in far:
        part = pick(keep, (mine + d) % 4) + swap_cores(pick(send, (partner + d) % 4))
        if d:
            part = permute(part, first_axis(d))
        total = part if total is None else total + part
    value, total = total, None
    for d in far:
        part = pick(value, (partner + d) % 4)
        if d:
            part = permute(part, second_axis(d))
        total = part if total is None else total + part
    value = total.reshape(NZ, 12, total.shape[-1])
    total = pick(value, z)
    for d in (4, 3, 5, 2, 6, 1, 7):
        total = total + permute(pick(value, (z + d) % NZ), z_axis(d))
    return total


def per_device(inputs, query_proj, key_proj, value_proj, grad_out):
    length, width = query_proj.shape
    factor = 1.0 / (math.sqrt(HEAD) * length * lax.axis_size(SEQ))
    me = coords(lax.axis_index(SEQ))
    core = me[3].astype(jnp.int32).reshape(1)
    keep, send = states(core, query_proj, key_proj, value_proj, grad_out)
    loc = local(query_proj, key_proj, value_proj, grad_out)
    own, other = entering(core, me, keep, send)
    keep, send = weight_terms(
        core, inputs, loc, key_proj, value_proj, grad_out, own, other, factor
    )
    summed = scatter_sum(me, keep, send)
    return (summed[:, :width], summed[:, width : 2 * width], summed[:, 2 * width :])


def solution(mesh):
    return jax.shard_map(
        per_device,
        mesh=mesh,
        in_specs=(P(SEQ, None),) * 5,
        out_specs=(P(SEQ, None),) * 3,
        check_vma=False,
    )
```

```python
import functools
import math

import jax
import jax.numpy as jnp
from jax import lax
from jax.experimental import pallas as pl
from jax.experimental.pallas import tpu as pltpu
from jax.sharding import PartitionSpec as P

HEAD = 96
WIDTH = 2 * HEAD
NY, NZ, NX, NC = 4, 8, 4, 2
SEQ = "seq"
F32 = jnp.float32
BF16 = jnp.bfloat16


def coords(i):
    return i >> 6, (i >> 3) & 7, (i >> 1) & 3, i & 1


def index(y, z, x, c):
    return ((y * NZ + z) * NX + x) * NC + c


def permute(value, move):
    pairs = []
    for i in range(NY * NZ * NX * NC):
        to = move(*coords(i))
        if to is not None:
            pairs.append((i, index(*to)))
    return lax.ppermute(value, SEQ, pairs)


def swap_cores(value):
    return permute(value, lambda y, z, x, c: (y, z, x, 1 - c))


def x_partner(m):
    return lambda y, z, x, c: (y, z, x ^ m, c)


def y_partner(m):
    return lambda y, z, x, c: (y ^ m, z, x, c)


def z_partner(m):
    return lambda y, z, x, c: (y, z ^ m, x, c)


def first_partner(m):
    return lambda y, z, x, c: (y, z, x ^ m, c) if c == 0 else (y ^ m, z, x, c)


def second_partner(m):
    return lambda y, z, x, c: (y ^ m, z, x, c) if c == 0 else (y, z, x ^ m, c)


def last_near(y, z, x, c):
    return (y, z, x, 1 - c) if z >> 2 == c else (y, z ^ 6, x, c)


def last_far(y, z, x, c):
    return None if z >> 2 == c else (y, z ^ 6, x, 1 - c)


def rows_dot(a, b):
    return lax.dot_general(a, b, (((0,), (0,)), ((), ())), preferred_element_type=F32)


def lanes_dot(a, b):
    return lax.dot_general(a, b, (((1,), (1,)), ((), ())), preferred_element_type=F32)


def dot(a, b):
    return jnp.dot(a, b, preferred_element_type=F32)


def head(array, h):
    return array[h * HEAD : (h + 1) * HEAD]


def states_kernel(place, q, k, v, g, keep, send):
    first = place[0] == 0
    for h in range(2):
        rows = slice(h * HEAD, (h + 1) * HEAD)
        key_state = lanes_dot(k[rows, :], v[rows, :])
        query_state = lanes_dot(q[rows, :], g[rows, :])
        keep[rows, :] = jnp.where(first, key_state, query_state)
        send[rows, :] = jnp.where(first, query_state, key_state)


def widen_kernel(q, k, v, g, out):
    for n, ref in enumerate((q, k, v, g)):
        out[n] = ref[...].astype(F32)


def widen_inputs_kernel(place, x, out):
    out[...] = x[...].astype(F32)


def local_kernel(place, q, k, v, g, other, local, outer):
    first = place[0] == 0
    mine = [ref[...] for ref in (q, k, v, g)]
    theirs = [other[n].astype(BF16) for n in range(4)]
    early = [jnp.where(first, a, b) for a, b in zip(mine, theirs)]
    late = [jnp.where(first, b, a) for a, b in zip(mine, theirs)]
    length = q.shape[1]
    s = lax.broadcasted_iota(jnp.int32, (length, length), 0)
    t = lax.broadcasted_iota(jnp.int32, (length, length), 1)
    causal = s <= t
    for core, (qt, kt, vt, gt) in enumerate((early, late)):
        outer[core, :, :] = jnp.zeros(outer.shape[1:], BF16)
        for n, a in enumerate((gt, vt, kt)):
            outer[core, n * 256 : n * 256 + WIDTH, :] = a
        for h in range(2):
            qh, kh, vh, gh = (head(a, h) for a in (qt, kt, vt, gt))
            vg = jnp.where(causal, rows_dot(vh, gh), 0.0).astype(BF16)
            kq = jnp.where(causal, rows_dot(kh, qh), 0.0).astype(BF16)
            dq = dot(kh, vg)
            dk = lanes_dot(qh, vg)
            dv = lanes_dot(gh, kq)
            if core == 0:
                state = lanes_dot(head(late[0], h), head(late[3], h)).astype(BF16)
                dk = dk + dot(state, vh)
                dv = dv + rows_dot(state, kh)
            else:
                state = lanes_dot(head(early[1], h), head(early[2], h)).astype(BF16)
                dq = dq + dot(state, gh)
            for n, a in enumerate((dq, dk, dv)):
                at = n * WIDTH + h * HEAD
                local[core, at : at + HEAD, :] = a.astype(BF16)


def terms_kernel(place, x, wide, local, outer, sums, high, low):
    c = place[0]
    theirs = wide[...].astype(BF16)
    mine = x[...]

    def over_tokens(d):
        contract = (((0,), (1,)), ((), ()))
        one = lax.dot_general(mine, d[c], contract, preferred_element_type=F32)
        return one + lax.dot_general(theirs, d[1 - c], contract, preferred_element_type=F32)

    shape = (1, 4, 96, -1)
    sums[...] = over_tokens(local).reshape(shape)
    outside = over_tokens(outer)
    top = outside.astype(BF16)
    high[...] = top.reshape(shape)
    low[...] = (outside - top.astype(F32)).astype(BF16).reshape(shape)


def join_kernel(factor, part, place, own, other, sums, high, low, keep, send):
    c, pa, pb, pz = (place[i] for i in range(4))
    first = c == 0
    row = lax.broadcasted_iota(jnp.int32, (WIDTH, WIDTH), 0) // HEAD
    col = lax.broadcasted_iota(jnp.int32, (WIDTH, WIDTH), 1) // HEAD

    def by_head(state):
        return jnp.where(row == col, jnp.concatenate([state, state], axis=1), 0.0).astype(BF16)

    before = by_head(jnp.where(first, own[...], other[...]))
    later = by_head(jnp.where(first, other[...], own[...]))

    def slot(p):
        order = (0, 1, 3, 2) if part == 0 else (0, 2, 3, 1)
        out = jnp.int32(0)
        for n in range(1, 4):
            out = jnp.where(p == n, order[n], out)
        return out

    for k in range(2):
        zi = pz ^ (k + 2 * part)

        for y in range(NY):
            pieces = []
            for n, (state, multiply) in enumerate(((before, lanes_dot), (later, lanes_dot), (later, dot))):
                lanes = slice(n * 256, n * 256 + WIDTH)
                total = sums[y, zi, :, n * WIDTH : (n + 1) * WIDTH]
                for ref in (high, low):
                    total = total + multiply(ref[y, zi, :, lanes], state)
                pieces.append(factor * total)
            value = jnp.concatenate(pieces, axis=1)
            for x in range(NX):
                sa = slot(jnp.where(first, x, y) ^ pa)
                sb = slot(jnp.where(first, y, x) ^ pb)
                rows = value[x * 24 : x * 24 + 24, :]

                @pl.when(sa < 2)
                def _(sa=sa, sb=sb, k=k, rows=rows):
                    keep[sa, sb, k] = rows

                @pl.when(sa >= 2)
                def _(sa=sa, sb=sb, k=k, rows=rows):
                    send[sa - 2, sb, k] = rows


VMEM = pl.BlockSpec(memory_space=pltpu.VMEM)
SMEM = pl.BlockSpec(memory_space=pltpu.SMEM)


def cost(flops, moved):
    return pl.CostEstimate(flops=flops, bytes_accessed=moved, transcendentals=0)


def limit(mib):
    return pltpu.CompilerParams(vmem_limit_bytes=mib * 2**20)


def states(place, q, k, v, g):
    shape = jax.ShapeDtypeStruct((WIDTH, HEAD), F32)
    return pl.pallas_call(
        states_kernel,
        name="states",
        out_shape=(shape, shape),
        in_specs=[SMEM] + [VMEM] * 4,
        out_specs=(VMEM, VMEM),
        cost_estimate=cost(4 * 512 * 192 * 192, 10**6),
    )(place, q, k, v, g)


def widen(q, k, v, g):
    return pl.pallas_call(
        widen_kernel,
        name="widen",
        out_shape=jax.ShapeDtypeStruct((4,) + q.shape, F32),
        in_specs=[VMEM] * 4,
        out_specs=VMEM,
        cost_estimate=cost(10**6, 24 * 10**5),
    )(q, k, v, g)


def widen_inputs(place, x):
    length, features = x.shape
    block = (length, features // 8)
    return pl.pallas_call(
        widen_inputs_kernel,
        name="widen_inputs",
        out_shape=jax.ShapeDtypeStruct((length, features // 2), F32),
        grid_spec=pltpu.PrefetchScalarGridSpec(
            num_scalar_prefetch=1,
            grid=(4,),
            in_specs=[pl.BlockSpec(block, lambda y, place: (0, 2 * y + 1 - place[0]))],
            out_specs=pl.BlockSpec(block, lambda y, place: (0, y)),
        ),
        cost_estimate=cost(10**6, 5 * 10**6),
    )(place, x)


def local_terms(place, q, k, v, g, other):
    length = q.shape[1]
    return pl.pallas_call(
        local_kernel,
        name="local_terms",
        out_shape=(
            jax.ShapeDtypeStruct((2, 3 * WIDTH, length), BF16),
            jax.ShapeDtypeStruct((2, 3 * 256, length), BF16),
        ),
        in_specs=[SMEM] + [VMEM] * 5,
        out_specs=(VMEM, VMEM),
        cost_estimate=cost(40 * 512 * 512 * 96, 5 * 10**6),
        compiler_params=limit(32),
    )(place, q, k, v, g, other)


def terms(place, x, wide, local, outer):
    length, features = x.shape
    block = (length, features // 8)
    whole = lambda a: pl.BlockSpec(a.shape, lambda y, place: (0,) * a.ndim)
    out = lambda lanes: pl.BlockSpec((1, 4, 96, lanes), lambda y, place: (y, 0, 0, 0))
    return pl.pallas_call(
        terms_kernel,
        name="terms",
        out_shape=(
            jax.ShapeDtypeStruct((4, 4, 96, 3 * WIDTH), F32),
            jax.ShapeDtypeStruct((4, 4, 96, 3 * 256), BF16),
            jax.ShapeDtypeStruct((4, 4, 96, 3 * 256), BF16),
        ),
        grid_spec=pltpu.PrefetchScalarGridSpec(
            num_scalar_prefetch=1,
            grid=(4,),
            in_specs=[
                pl.BlockSpec(block, lambda y, place: (0, 2 * y + place[0])),
                pl.BlockSpec(block, lambda y, place: (0, y)),
                whole(local),
                whole(outer),
            ],
            out_specs=(out(3 * WIDTH), out(3 * 256), out(3 * 256)),
        ),
        cost_estimate=cost(4 * 512 * 3072 * 576, 12 * 10**6),
        compiler_params=limit(32),
    )(place, x, wide, local, outer)


def join(part, factor, place, own, other, sums, high, low):
    shape = jax.ShapeDtypeStruct((2, 4, 2, 24, 3 * WIDTH), F32)
    return pl.pallas_call(
        functools.partial(join_kernel, factor, part),
        name=f"join{part}",
        out_shape=(shape, shape),
        in_specs=[SMEM] + [VMEM] * 5,
        out_specs=(VMEM, VMEM),
        cost_estimate=cost(12 * 768 * 192 * 192, 10**7),
        compiler_params=limit(32),
    )(place, own, other, sums, high, low)


def before_chip(me, total):
    y, z, x, c = me
    before = jnp.zeros_like(total)
    steps = (
        (x_partner(1), x & 1),
        (x_partner(3), x >> 1),
        (z_partner(1), z & 1),
        (z_partner(2), (z >> 1) & 1),
        (z_partner(6), z >> 2),
        (y_partner(1), y & 1),
        (y_partner(3), y >> 1),
    )
    for move, bit in steps:
        came = permute(total, move)
        before = before + jnp.where(bit != c, came, 0.0)
        total = total + came
    return before


def halve(keep, send, move_one, move_two):
    came = permute(send, move_one)
    return keep[0] + came[0] + permute(keep[1] + came[1], move_two)


def scatter_sum(me, parts):
    y, z, x, c = me
    ends = []
    for (keep, send), (one, two) in zip(parts, ((3, 1), (1, 3))):
        value = halve(keep, send, first_partner(one), first_partner(two))
        ends.append(halve(value[:2], value[2:], second_partner(one), second_partner(two)))
    value = ends[0] + permute(ends[1], z_partner(2))
    value = value[0] + permute(value[1], z_partner(1))
    block = lambda i: jnp.where(i == 0, value[:12], value[12:])
    same = z >> 2 == c
    total = jnp.where(same, block(c), 0.0)
    total = total + permute(block(jnp.where(same, 1 - c, c)), last_near)
    return total + permute(block(1 - c), last_far)


def per_device(inputs, query_proj, key_proj, value_proj, grad_out):
    length, width = query_proj.shape
    factor = 1.0 / (math.sqrt(HEAD) * length * lax.axis_size(SEQ))
    me = coords(lax.axis_index(SEQ))
    y, z, x, c = me
    block = (z & 3) ^ jnp.where(z >> 2 == c, 0, 2)
    place = jnp.stack([c, jnp.where(c == 0, x, y), jnp.where(c == 0, y, x), block]).astype(jnp.int32)
    features_first = [a.T for a in (query_proj, key_proj, value_proj, grad_out)]
    keep, send = states(place, *features_first)
    before = before_chip(me, keep + swap_cores(send))
    other = swap_cores(widen(*features_first))
    wide = swap_cores(widen_inputs(place, inputs))
    local, outer = local_terms(place, *features_first, other)
    pieces = terms(place, inputs, wide, local, outer)
    across = swap_cores(before)
    parts = [join(part, factor, place, before, across, *pieces) for part in range(2)]
    summed = scatter_sum(me, parts)
    return (summed[:, :width], summed[:, width : 2 * width], summed[:, 2 * width :])


def solution(mesh):
    return jax.shard_map(
        per_device,
        mesh=mesh,
        in_specs=(P(SEQ, None),) * 5,
        out_specs=(P(SEQ, None),) * 3,
        check_vma=False,
    )
```

```python
import functools
import math

import jax
import jax.numpy as jnp
from jax import lax
from jax.experimental import pallas as pl
from jax.experimental.pallas import tpu as pltpu
from jax.sharding import PartitionSpec as P

HEAD = 96
WIDTH = 2 * HEAD
NY, NZ, NX, NC = 4, 8, 4, 2
SEQ = "seq"
F32 = jnp.float32
BF16 = jnp.bfloat16


def coords(i):
    return i >> 6, (i >> 3) & 7, (i >> 1) & 3, i & 1


def index(y, z, x, c):
    return ((y * NZ + z) * NX + x) * NC + c


def permute(value, move):
    pairs = []
    for i in range(NY * NZ * NX * NC):
        to = move(*coords(i))
        if to is not None:
            pairs.append((i, index(*to)))
    return lax.ppermute(value, SEQ, pairs)


def swap_cores(value):
    return permute(value, lambda y, z, x, c: (y, z, x, 1 - c))


def x_partner(m):
    return lambda y, z, x, c: (y, z, x ^ m, c)


def y_partner(m):
    return lambda y, z, x, c: (y ^ m, z, x, c)


def z_partner(m):
    return lambda y, z, x, c: (y, z ^ m, x, c)


def first_partner(m):
    return lambda y, z, x, c: (y, z, x ^ m, c) if c == 0 else (y ^ m, z, x, c)


def second_partner(m):
    return lambda y, z, x, c: (y ^ m, z, x, c) if c == 0 else (y, z, x ^ m, c)


def last_near(y, z, x, c):
    return (y, z, x, 1 - c) if z >> 2 == c else (y, z ^ 6, x, c)


def last_far(y, z, x, c):
    return None if z >> 2 == c else (y, z ^ 6, x, 1 - c)


def rows_dot(a, b):
    return lax.dot_general(a, b, (((0,), (0,)), ((), ())), preferred_element_type=F32)


def lanes_dot(a, b):
    return lax.dot_general(a, b, (((1,), (1,)), ((), ())), preferred_element_type=F32)


def dot(a, b):
    return jnp.dot(a, b, preferred_element_type=F32)


def head(array, h):
    return array[h * HEAD : (h + 1) * HEAD]


PACKED = (144, 128)


def pack(pair, ref):
    ref[0:96, 0:96] = pair[0]
    ref[0:96, 96:128] = pair[1][:, 0:32]
    ref[96:144, 0:64] = pair[1][0:48, 32:96]
    ref[96:144, 64:128] = pair[1][48:96, 32:96]


def unpack(array):
    rest = jnp.concatenate([array[96:144, 0:64], array[96:144, 64:128]], axis=0)
    return array[0:96, 0:96], jnp.concatenate([array[0:96, 96:128], rest], axis=1)


def states_kernel(place, *refs):
    sources, (keep, send), held, arrived = refs[:4], refs[4:6], refs[6:10], refs[10]
    copies = [pltpu.make_async_copy(a, b, arrived.at[n]) for n, (a, b) in enumerate(zip(sources, held))]
    for copy in copies:
        copy.start()
    for copy in copies:
        copy.wait()
    q, k, v, g = held
    first = place[0] == 0
    key_state = [lanes_dot(head(k[...], h), head(v[...], h)) for h in range(2)]
    query_state = [lanes_dot(head(q[...], h), head(g[...], h)) for h in range(2)]
    pack([jnp.where(first, a, b) for a, b in zip(key_state, query_state)], keep)
    pack([jnp.where(first, b, a) for a, b in zip(key_state, query_state)], send)


def widen_kernel(q, k, v, g, out):
    for n, ref in enumerate((q, k, v, g)):
        out[n] = ref[...].astype(F32)


def widen_inputs_kernel(place, x, out):
    out[...] = x[...].astype(F32)


def local_kernel(place, q, k, v, g, other, local, outer):
    first = place[0] == 0
    mine = [ref[...] for ref in (q, k, v, g)]
    theirs = [other[n].astype(BF16) for n in range(4)]
    early = [jnp.where(first, a, b) for a, b in zip(mine, theirs)]
    late = [jnp.where(first, b, a) for a, b in zip(mine, theirs)]
    length = q.shape[1]
    s = lax.broadcasted_iota(jnp.int32, (length, length), 0)
    t = lax.broadcasted_iota(jnp.int32, (length, length), 1)
    causal = s <= t
    for core, (qt, kt, vt, gt) in enumerate((early, late)):
        outer[core, :, :] = jnp.zeros(outer.shape[1:], BF16)
        for n, a in enumerate((gt, vt, kt)):
            outer[core, n * 256 : n * 256 + WIDTH, :] = a
        for h in range(2):
            qh, kh, vh, gh = (head(a, h) for a in (qt, kt, vt, gt))
            vg = jnp.where(causal, rows_dot(vh, gh), 0.0).astype(BF16)
            kq = jnp.where(causal, rows_dot(kh, qh), 0.0).astype(BF16)
            dq = dot(kh, vg)
            dk = lanes_dot(qh, vg)
            dv = lanes_dot(gh, kq)
            if core == 0:
                state = lanes_dot(head(late[0], h), head(late[3], h)).astype(BF16)
                dk = dk + dot(state, vh)
                dv = dv + rows_dot(state, kh)
            else:
                state = lanes_dot(head(early[1], h), head(early[2], h)).astype(BF16)
                dq = dq + dot(state, gh)
            for n, a in enumerate((dq, dk, dv)):
                at = n * WIDTH + h * HEAD
                local[core, at : at + HEAD, :] = a.astype(BF16)


def over_tokens(place, x, wide, d):
    c = place[0]
    contract = (((0,), (1,)), ((), ()))
    one = lax.dot_general(x[...], d[c], contract, preferred_element_type=F32)
    theirs = wide[...].astype(BF16)
    return one + lax.dot_general(theirs, d[1 - c], contract, preferred_element_type=F32)


def inner_terms_kernel(place, x, wide, local, sums):
    sums[...] = over_tokens(place, x, wide, local).reshape(sums.shape)


def outer_terms_kernel(place, x, wide, outer, high, low):
    outside = over_tokens(place, x, wide, outer)
    top = outside.astype(BF16)
    high[...] = top.reshape(high.shape)
    low[...] = (outside - top.astype(F32)).astype(BF16).reshape(low.shape)


def join_kernel(factor, part, place, own, other, sums, high, low, keep, send):
    c, pa, pb = (place[i] for i in range(3))
    first = c == 0

    def by_head(state):
        one, two = unpack(state)
        none = jnp.zeros_like(one)
        rows = [jnp.concatenate(pair, axis=1) for pair in ((one, none), (none, two))]
        return jnp.concatenate(rows, axis=0).astype(BF16)

    before = by_head(jnp.where(first, own[...], other[...]))
    later = by_head(jnp.where(first, other[...], own[...]))

    def slot(p):
        order = (0, 1, 3, 2) if part == 0 else (0, 2, 3, 1)
        out = jnp.int32(0)
        for n in range(1, 4):
            out = jnp.where(p == n, order[n], out)
        return out

    pieces = []
    for n, (state, multiply) in enumerate(((before, lanes_dot), (later, lanes_dot), (later, dot))):
        total = sums[:, 0, :, n * WIDTH : (n + 1) * WIDTH].reshape(4 * 96, WIDTH)
        for ref in (high, low):
            term = ref[:, 0, :, n * 256 : n * 256 + WIDTH].reshape(4 * 96, WIDTH)
            total = total + multiply(term, state)
        pieces.append(factor * total)
    value = jnp.concatenate(pieces, axis=1)
    for y in range(NY):
        for x in range(NX):
            sa = slot(jnp.where(first, x, y) ^ pa)
            sb = slot(jnp.where(first, y, x) ^ pb)
            at = y * 96 + x * 24
            rows = value[at : at + 24, :]

            @pl.when(sa < 2)
            def _(sa=sa, sb=sb, rows=rows):
                keep[sa, sb, 0] = rows

            @pl.when(sa >= 2)
            def _(sa=sa, sb=sb, rows=rows):
                send[sa - 2, sb, 0] = rows


VMEM = pl.BlockSpec(memory_space=pltpu.VMEM)
SMEM = pl.BlockSpec(memory_space=pltpu.SMEM)


def cost(flops, moved):
    return pl.CostEstimate(flops=flops, bytes_accessed=moved, transcendentals=0)


def limit(mib):
    return pltpu.CompilerParams(vmem_limit_bytes=mib * 2**20)


def states(place, q, k, v, g):
    shape = jax.ShapeDtypeStruct(PACKED, F32)
    return pl.pallas_call(
        states_kernel,
        name="states",
        out_shape=(shape, shape),
        in_specs=[SMEM] + [pl.BlockSpec(memory_space=pltpu.HBM)] * 4,
        out_specs=(VMEM, VMEM),
        scratch_shapes=[pltpu.VMEM(q.shape, BF16)] * 4 + [pltpu.SemaphoreType.DMA((4,))],
        cost_estimate=cost(4 * 512 * 192 * 192, 10**6),
    )(place, q, k, v, g)


def widen(q, k, v, g):
    return pl.pallas_call(
        widen_kernel,
        name="widen",
        out_shape=jax.ShapeDtypeStruct((4,) + q.shape, F32),
        in_specs=[VMEM] * 4,
        out_specs=VMEM,
        cost_estimate=cost(10**6, 24 * 10**5),
    )(q, k, v, g)


def widen_inputs(place, x):
    length, features = x.shape
    block = (length, features // 8)
    return pl.pallas_call(
        widen_inputs_kernel,
        name="widen_inputs",
        out_shape=jax.ShapeDtypeStruct((length, features // 2), F32),
        grid_spec=pltpu.PrefetchScalarGridSpec(
            num_scalar_prefetch=1,
            grid=(4,),
            in_specs=[pl.BlockSpec(block, lambda y, place: (0, 2 * y + 1 - place[0]))],
            out_specs=pl.BlockSpec(block, lambda y, place: (0, y)),
        ),
        cost_estimate=cost(10**6, 5 * 10**6),
    )(place, x)


def local_terms(place, q, k, v, g, other):
    length = q.shape[1]
    return pl.pallas_call(
        local_kernel,
        name="local_terms",
        out_shape=(
            jax.ShapeDtypeStruct((2, 3 * WIDTH, length), BF16),
            jax.ShapeDtypeStruct((2, 3 * 256, length), BF16),
        ),
        in_specs=[SMEM] + [VMEM] * 5,
        out_specs=(VMEM, VMEM),
        cost_estimate=cost(40 * 512 * 512 * 96, 5 * 10**6),
        compiler_params=limit(32),
    )(place, q, k, v, g, other)


def terms(kernel, place, x, wide, d, types):
    length, features = x.shape
    lanes = d.shape[1]
    block = (length, features // 8)
    out = pl.BlockSpec((1, 4, 96, lanes), lambda y, place: (y, 0, 0, 0))
    return pl.pallas_call(
        kernel,
        name=kernel.__name__,
        out_shape=tuple(jax.ShapeDtypeStruct((4, 4, 96, lanes), t) for t in types),
        grid_spec=pltpu.PrefetchScalarGridSpec(
            num_scalar_prefetch=1,
            grid=(4,),
            in_specs=[
                pl.BlockSpec(block, lambda y, place: (0, 2 * y + place[0])),
                pl.BlockSpec(block, lambda y, place: (0, y)),
                pl.BlockSpec(d.shape, lambda y, place: (0, 0, 0)),
            ],
            out_specs=(out,) * len(types),
        ),
        cost_estimate=cost(2 * 512 * 3072 * 576, 8 * 10**6),
        compiler_params=limit(24),
    )(place, x, wide, d)


def join(part, factor, place, own, other, sums, high, low):
    shape = jax.ShapeDtypeStruct((2, 4, 2, 24, 3 * WIDTH), F32)
    state = pl.BlockSpec(PACKED, lambda k, place: (0, 0))
    block = lambda lanes: pl.BlockSpec(
        (4, 1, 96, lanes), lambda k, place: (0, place[3] ^ (k + 2 * part), 0, 0)
    )
    out = pl.BlockSpec((2, 4, 1, 24, 3 * WIDTH), lambda k, place: (0, 0, k, 0, 0))
    return pl.pallas_call(
        functools.partial(join_kernel, factor, part),
        name=f"join{part}",
        out_shape=(shape, shape),
        grid_spec=pltpu.PrefetchScalarGridSpec(
            num_scalar_prefetch=1,
            grid=(2,),
            in_specs=[state, state, block(3 * WIDTH), block(3 * 256), block(3 * 256)],
            out_specs=(out, out),
        ),
        cost_estimate=cost(12 * 768 * 192 * 192, 8 * 10**6),
        compiler_params=limit(24),
    )(place, own, other, sums, high, low)


def tie(*values):
    return lax.optimization_barrier(values)


def before_chip(me, total, works):
    y, z, x, c = me
    before = jnp.zeros_like(total)
    steps = (
        (x_partner(1), x & 1),
        (x_partner(3), x >> 1),
        (z_partner(1), z & 1),
        (z_partner(2), (z >> 1) & 1),
        (z_partner(6), z >> 2),
        (y_partner(1), y & 1),
        (y_partner(3), y >> 1),
    )
    for n, (move, bit) in enumerate(steps):
        came = permute(total, move)
        if n < len(works):
            came, total = works[n](came, total)
        before = before + jnp.where(bit != c, came, 0.0)
        total = total + came
    return before


def halve(keep, send, move_one, move_two):
    came = permute(send, move_one)
    return keep[0] + came[0] + permute(keep[1] + came[1], move_two)


def scatter_sum(me, parts):
    y, z, x, c = me
    ends = []
    for (keep, send), (one, two) in zip(parts, ((3, 1), (1, 3))):
        value = halve(keep, send, first_partner(one), first_partner(two))
        ends.append(halve(value[:2], value[2:], second_partner(one), second_partner(two)))
    value = ends[0] + permute(ends[1], z_partner(2))
    value = value[0] + permute(value[1], z_partner(1))
    block = lambda i: jnp.where(i == 0, value[:12], value[12:])
    same = z >> 2 == c
    total = jnp.where(same, block(c), 0.0)
    total = total + permute(block(jnp.where(same, 1 - c, c)), last_near)
    return total + permute(block(1 - c), last_far)


def per_device(inputs, query_proj, key_proj, value_proj, grad_out):
    length, width = query_proj.shape
    factor = 1.0 / (math.sqrt(HEAD) * length * lax.axis_size(SEQ))
    me = coords(lax.axis_index(SEQ))
    y, z, x, c = me
    block = (z & 3) ^ jnp.where(z >> 2 == c, 0, 2)
    place = jnp.stack([c, jnp.where(c == 0, x, y), jnp.where(c == 0, y, x), block]).astype(jnp.int32)
    features_first = [a.T for a in (query_proj, key_proj, value_proj, grad_out)]
    keep, send = states(place, *features_first)
    send, *late = tie(send, *features_first)
    came = swap_cores(send)
    plain = widen(*late)
    came, plain = tie(came, plain)
    other = swap_cores(plain)
    made = {}

    def inputs_work(came, total):
        total, x = tie(total, inputs)
        came, wide = tie(came, widen_inputs(place, x))
        made["wide"] = swap_cores(wide)
        return came, total

    def local_work(came, total):
        total, theirs = tie(total, other)
        came, *made["local"] = tie(came, *local_terms(place, *late, theirs))
        return came, total

    def outer_work(came, total):
        total, d = tie(total, made["local"][1])
        kernel = outer_terms_kernel
        came, *made["outer"] = tie(came, *terms(kernel, place, inputs, made["wide"], d, (BF16, BF16)))
        return came, total

    def inner_work(came, total):
        total, d = tie(total, made["local"][0])
        came, made["inner"] = tie(came, *terms(inner_terms_kernel, place, inputs, made["wide"], d, (F32,)))
        return came, total

    before = before_chip(me, keep + came, (inputs_work, local_work, outer_work, inner_work))
    across = swap_cores(before)
    parts = [
        join(part, factor, place, before, across, made["inner"], *made["outer"]) for part in range(2)
    ]
    summed = scatter_sum(me, parts)
    return (summed[:, :width], summed[:, width : 2 * width], summed[:, 2 * width :])


def solution(mesh):
    return jax.shard_map(
        per_device,
        mesh=mesh,
        in_specs=(P(SEQ, None),) * 5,
        out_specs=(P(SEQ, None),) * 3,
        check_vma=False,
    )
```

```python
import functools
import math

import jax
import jax.numpy as jnp
from jax import lax
from jax.experimental import pallas as pl
from jax.experimental.pallas import tpu as pltpu
from jax.sharding import PartitionSpec as P

HEAD = 96
WIDTH = 2 * HEAD
NY, NZ, NX, NC = 4, 8, 4, 2
SEQ = "seq"
F32 = jnp.float32
BF16 = jnp.bfloat16


def coords(i):
    return i >> 6, (i >> 3) & 7, (i >> 1) & 3, i & 1


def index(y, z, x, c):
    return ((y * NZ + z) * NX + x) * NC + c


def permute(value, move):
    pairs = []
    for i in range(NY * NZ * NX * NC):
        to = move(*coords(i))
        if to is not None:
            pairs.append((i, index(*to)))
    return lax.ppermute(value, SEQ, pairs)


def swap_cores(value):
    return permute(value, lambda y, z, x, c: (y, z, x, 1 - c))


def x_partner(m):
    return lambda y, z, x, c: (y, z, x ^ m, c)


def y_partner(m):
    return lambda y, z, x, c: (y ^ m, z, x, c)


def z_partner(m):
    return lambda y, z, x, c: (y, z ^ m, x, c)


def first_partner(m):
    return lambda y, z, x, c: (y, z, x ^ m, c) if c == 0 else (y ^ m, z, x, c)


def second_partner(m):
    return lambda y, z, x, c: (y ^ m, z, x, c) if c == 0 else (y, z, x ^ m, c)


def last_near(y, z, x, c):
    return (y, z, x, 1 - c) if z >> 2 == c else (y, z ^ 6, x, c)


def last_far(y, z, x, c):
    return None if z >> 2 == c else (y, z ^ 6, x, 1 - c)


def rows_dot(a, b):
    return lax.dot_general(a, b, (((0,), (0,)), ((), ())), preferred_element_type=F32)


def lanes_dot(a, b):
    return lax.dot_general(a, b, (((1,), (1,)), ((), ())), preferred_element_type=F32)


def dot(a, b):
    return jnp.dot(a, b, preferred_element_type=F32)


def head(array, h):
    return array[h * HEAD : (h + 1) * HEAD]


PACKED = (144, 128)


def pack(pair, ref):
    ref[0:96, 0:96] = pair[0]
    ref[0:96, 96:128] = pair[1][:, 0:32]
    ref[96:144, 0:64] = pair[1][0:48, 32:96]
    ref[96:144, 64:128] = pair[1][48:96, 32:96]


def unpack(array):
    rest = jnp.concatenate([array[96:144, 0:64], array[96:144, 64:128]], axis=0)
    return array[0:96, 0:96], jnp.concatenate([array[0:96, 96:128], rest], axis=1)


def states_kernel(*refs):
    sources, (keep, send), held, arrived = refs[:4], refs[4:6], refs[6:10], refs[10]
    copies = [pltpu.make_async_copy(a, b, arrived.at[n]) for n, (a, b) in enumerate(zip(sources, held))]
    for copy in copies:
        copy.start()
    for copy in copies:
        copy.wait()
    q, k, v, g = held
    first = lax.axis_index(SEQ) & 1 == 0
    key_state = [lanes_dot(head(k[...], h), head(v[...], h)) for h in range(2)]
    query_state = [lanes_dot(head(q[...], h), head(g[...], h)) for h in range(2)]
    pack([jnp.where(first, a, b) for a, b in zip(key_state, query_state)], keep)
    pack([jnp.where(first, b, a) for a, b in zip(key_state, query_state)], send)


def widen_kernel(q, k, v, g, out):
    for n, ref in enumerate((q, k, v, g)):
        out[n] = ref[...].astype(F32)


def widen_inputs_kernel(place, x, out, held, arrived):
    lanes = held.shape[2]
    copies = []
    for y in range(NY):
        at = pl.multiple_of((2 * y + 1 - place[0]) * lanes, 128)
        copies.append(pltpu.make_async_copy(x.at[:, pl.ds(at, lanes)], held.at[y], arrived.at[y]))
        copies[y].start()
    for y in range(NY):
        copies[y].wait()
        out[y] = held[y].astype(F32)


def local_kernel(place, q, k, v, g, other, local, outer):
    first = place[0] == 0
    mine = [ref[...] for ref in (q, k, v, g)]
    theirs = [other[n].astype(BF16) for n in range(4)]
    early = [jnp.where(first, a, b) for a, b in zip(mine, theirs)]
    late = [jnp.where(first, b, a) for a, b in zip(mine, theirs)]
    length = q.shape[1]
    s = lax.broadcasted_iota(jnp.int32, (length, length), 0)
    t = lax.broadcasted_iota(jnp.int32, (length, length), 1)
    causal = s <= t
    for core, (qt, kt, vt, gt) in enumerate((early, late)):
        outer[core, :, :] = jnp.zeros(outer.shape[1:], BF16)
        for n, a in enumerate((gt, vt, kt)):
            outer[core, n * 256 : n * 256 + WIDTH, :] = a
        for h in range(2):
            qh, kh, vh, gh = (head(a, h) for a in (qt, kt, vt, gt))
            vg = jnp.where(causal, rows_dot(vh, gh), 0.0).astype(BF16)
            kq = jnp.where(causal, rows_dot(kh, qh), 0.0).astype(BF16)
            dq = dot(kh, vg)
            dk = lanes_dot(qh, vg)
            dv = lanes_dot(gh, kq)
            if core == 0:
                state = lanes_dot(head(late[0], h), head(late[3], h)).astype(BF16)
                dk = dk + dot(state, vh)
                dv = dv + rows_dot(state, kh)
            else:
                state = lanes_dot(head(early[1], h), head(early[2], h)).astype(BF16)
                dq = dq + dot(state, gh)
            for n, a in enumerate((dq, dk, dv)):
                at = n * WIDTH + h * HEAD
                local[core, at : at + HEAD, :] = a.astype(BF16)


def terms_kernel(inner, place, x, wide, d, out, held):
    c, pa, pb, pz = (place[i] for i in range(4))
    first = c == 0
    y = pl.program_id(0)
    contract = (((0,), (1,)), ((), ()))
    total = lax.dot_general(x[...], d[c], contract, preferred_element_type=F32)
    theirs = wide[0].astype(BF16)
    total = total + lax.dot_general(theirs, d[1 - c], contract, preferred_element_type=F32)
    held[...] = total.reshape(held.shape)

    def slot(p, order):
        at = jnp.int32(0)
        for n in range(1, 4):
            at = jnp.where(p == n, order[n], at)
        return at

    for part in range(2):
        pair = [pz ^ (2 * part + k) for k in range(2)]
        for x_to in range(NX):
            sa = slot(jnp.where(first, x_to, y) ^ pa, ((0, 1, 3, 2), (0, 2, 3, 1))[part])
            sb = jnp.where(first, y, x_to) ^ pb
            sides = []
            for side in range(2):
                rows = slice(x_to * 24 + side * 12, x_to * 24 + side * 12 + 12)
                sides.append(jnp.concatenate([held[z, rows, :] for z in pair], axis=0))
            if inner:
                out[part, sa, sb] = jnp.concatenate(sides, axis=1)
            else:
                out[part, sa, sb, 0] = sides[0]
                out[part, sa, sb, 1] = sides[1]


def join_kernel(factor, part, half, place, own, other, inner, outer, out):
    first = place[0] == 0

    def by_head(state):
        one, two = unpack(state)
        none = jnp.zeros_like(one)
        rows = [jnp.concatenate(pair, axis=1) for pair in ((one, none), (none, two))]
        return jnp.concatenate(rows, axis=0).astype(BF16)

    before = by_head(jnp.where(first, own[...], other[...]))
    later = by_head(jnp.where(first, other[...], own[...]))
    for sa in range(2):
        pieces = []
        for side in range(2):
            for n, (state, multiply) in enumerate(((before, lanes_dot), (later, lanes_dot), (later, dot))):
                term = outer[part, 2 * half + sa, :, side, :, n * 256 : n * 256 + WIDTH]
                term = term.reshape(4 * 24, WIDTH)
                high = term.astype(BF16)
                low = (term - high.astype(F32)).astype(BF16)
                pieces.append(multiply(high, state) + multiply(low, state))
        total = jnp.concatenate(pieces, axis=1).reshape(4, 24, 6 * WIDTH)
        out[sa] = factor * (inner[part, 2 * half + sa] + total)


VMEM = pl.BlockSpec(memory_space=pltpu.VMEM)
SMEM = pl.BlockSpec(memory_space=pltpu.SMEM)
HBM = pl.BlockSpec(memory_space=pltpu.HBM)


def cost(flops, moved):
    return pl.CostEstimate(flops=flops, bytes_accessed=moved, transcendentals=0)


def limit(mib):
    return pltpu.CompilerParams(vmem_limit_bytes=mib * 2**20)


def states(q, k, v, g):
    shape = jax.ShapeDtypeStruct(PACKED, F32)
    return pl.pallas_call(
        states_kernel,
        name="states",
        out_shape=(shape, shape),
        in_specs=[HBM] * 4,
        out_specs=(VMEM, VMEM),
        scratch_shapes=[pltpu.VMEM(q.shape, BF16)] * 4 + [pltpu.SemaphoreType.DMA((4,))],
        cost_estimate=cost(4 * 512 * 192 * 192, 10**6),
    )(q, k, v, g)


def widen(q, k, v, g):
    return pl.pallas_call(
        widen_kernel,
        name="widen",
        out_shape=jax.ShapeDtypeStruct((4,) + q.shape, F32),
        in_specs=[VMEM] * 4,
        out_specs=VMEM,
        cost_estimate=cost(10**6, 24 * 10**5),
    )(q, k, v, g)


def widen_inputs(place, x):
    length, features = x.shape
    shape = (NY, length, features // 8)
    return pl.pallas_call(
        widen_inputs_kernel,
        name="widen_inputs",
        out_shape=jax.ShapeDtypeStruct(shape, F32),
        in_specs=[SMEM, HBM],
        out_specs=VMEM,
        scratch_shapes=[pltpu.VMEM(shape, BF16), pltpu.SemaphoreType.DMA((NY,))],
        cost_estimate=cost(10**6, 5 * 10**6),
        compiler_params=limit(16),
    )(place, x)


def local_terms(place, q, k, v, g, other):
    length = q.shape[1]
    return pl.pallas_call(
        local_kernel,
        name="local_terms",
        out_shape=(
            jax.ShapeDtypeStruct((2, 3 * WIDTH, length), BF16),
            jax.ShapeDtypeStruct((2, 3 * 256, length), BF16),
        ),
        in_specs=[SMEM] + [VMEM] * 5,
        out_specs=(VMEM, VMEM),
        cost_estimate=cost(40 * 512 * 512 * 96, 5 * 10**6),
        compiler_params=limit(32),
    )(place, q, k, v, g, other)


def terms(inner, place, x, wide, d):
    length, features = x.shape
    lanes = d.shape[1]
    block = (length, features // 8)
    shape = (2, 4, 4, 24, 2 * lanes) if inner else (2, 4, 4, 2, 24, lanes)
    return pl.pallas_call(
        functools.partial(terms_kernel, inner),
        name="inner_terms" if inner else "outer_terms",
        out_shape=jax.ShapeDtypeStruct(shape, F32),
        grid_spec=pltpu.PrefetchScalarGridSpec(
            num_scalar_prefetch=1,
            grid=(4,),
            in_specs=[
                pl.BlockSpec(block, lambda y, place: (0, 2 * y + place[0])),
                pl.BlockSpec((1,) + block, lambda y, place: (y, 0, 0)),
                pl.BlockSpec(d.shape, lambda y, place: (0, 0, 0)),
            ],
            out_specs=pl.BlockSpec(shape, lambda y, place: (0,) * len(shape)),
            scratch_shapes=[pltpu.VMEM((4, 96, lanes), F32)],
        ),
        cost_estimate=cost(2 * 512 * 3072 * 576, 8 * 10**6),
        compiler_params=limit(24),
    )(place, x, wide, d)


def join(part, half, factor, place, own, other, inner, outer):
    return pl.pallas_call(
        functools.partial(join_kernel, factor, part, half),
        name=f"join{part}{half}",
        out_shape=jax.ShapeDtypeStruct((2, 4, 24, 6 * WIDTH), F32),
        in_specs=[SMEM] + [VMEM] * 4,
        out_specs=VMEM,
        cost_estimate=cost(12 * 384 * 192 * 192, 4 * 10**6),
        compiler_params=limit(20),
    )(place, own, other, inner, outer)


def tie(*values):
    return lax.optimization_barrier(values)


def before_chip(me, total, works):
    y, z, x, c = me
    before = jnp.zeros_like(total)
    steps = (
        (x_partner(1), x & 1),
        (x_partner(3), x >> 1),
        (z_partner(1), z & 1),
        (z_partner(2), (z >> 1) & 1),
        (z_partner(6), z >> 2),
        (y_partner(1), y & 1),
        (y_partner(3), y >> 1),
    )
    for n, (move, bit) in enumerate(steps):
        came = permute(total, move)
        if n < len(works) and works[n]:
            came, total = works[n](came, total)
        before = before + jnp.where(bit != c, came, 0.0)
        total = total + came
    return before


def halve(keep, send, move_one, move_two):
    came = permute(send, move_one)
    return keep[0] + came[0] + permute(keep[1] + came[1], move_two)


def scatter_sum(me, parts):
    y, z, x, c = me
    ends = []
    for (keep, send), (one, two) in zip(parts, ((3, 1), (1, 3))):
        ends.append(halve(keep, send, first_partner(one), first_partner(two)))
    chunk = lambda r: jnp.stack([end[r] for end in ends])
    value = chunk(0)
    for r in (2, 1, 3):
        value = value + permute(chunk(r), second_partner(r))
    chunk = lambda r: value[r >> 1, 12 * (r & 1) : 12 * (r & 1) + 12]
    total = chunk(0)
    for r in (3, 2, 1):
        total = total + permute(chunk(r), z_partner(r))
    left, right = jnp.split(total, 2, axis=1)
    block = lambda i: jnp.where(i == 0, left, right)
    same = z >> 2 == c
    total = jnp.where(same, block(c), 0.0)
    total = total + permute(block(jnp.where(same, 1 - c, c)), last_near)
    return total + permute(block(1 - c), last_far)


def per_device(inputs, query_proj, key_proj, value_proj, grad_out):
    length, width = query_proj.shape
    factor = 1.0 / (math.sqrt(HEAD) * length * lax.axis_size(SEQ))
    me = coords(lax.axis_index(SEQ))
    y, z, x, c = me
    block = (z & 3) ^ jnp.where(z >> 2 == c, 0, 2)
    place = jnp.stack([c, jnp.where(c == 0, x, y), jnp.where(c == 0, y, x), block]).astype(jnp.int32)
    features_first = [a.T for a in (query_proj, key_proj, value_proj, grad_out)]
    keep, send = states(*features_first)
    send, *late = tie(send, *features_first)
    came = swap_cores(send)
    plain = widen(*late)
    came, plain = tie(came, plain)
    other = swap_cores(plain)
    made = {}

    def inputs_work(came, total):
        total, x = tie(total, inputs)
        came, wide = tie(came, widen_inputs(place, x))
        made["wide"] = swap_cores(wide)
        return came, total

    def local_work(came, total):
        total, theirs = tie(total, other)
        came, *made["local"] = tie(came, *local_terms(place, *late, theirs))
        return came, total

    def outer_work(came, total):
        total, d = tie(total, made["local"][1])
        came, made["outer"] = tie(came, terms(False, place, inputs, made["wide"], d))
        return came, total

    def inner_work(came, total):
        total, d = tie(total, made["local"][0])
        came, made["inner"] = tie(came, terms(True, place, inputs, made["wide"], d))
        return came, total

    works = (inputs_work, None, local_work, outer_work, inner_work)
    before = before_chip(me, keep + came, works)
    across = swap_cores(before)
    joined = lambda part, half: join(
        part, half, factor, place, before, across, made["inner"], made["outer"]
    )
    parts = [(joined(part, 0), joined(part, 1)) for part in range(2)]
    summed = scatter_sum(me, parts)
    return (summed[:, :width], summed[:, width : 2 * width], summed[:, 2 * width :])


def solution(mesh):
    return jax.shard_map(
        per_device,
        mesh=mesh,
        in_specs=(P(SEQ, None),) * 5,
        out_specs=(P(SEQ, None),) * 3,
        check_vma=False,
    )
```

```python
import functools
import math

import jax
import jax.numpy as jnp
from jax import lax
from jax.experimental import pallas as pl
from jax.experimental.pallas import tpu as pltpu
from jax.sharding import PartitionSpec as P

HEAD = 96
WIDTH = 2 * HEAD
NY, NZ, NX, NC = 4, 8, 4, 2
SEQ = "seq"
F32 = jnp.float32
BF16 = jnp.bfloat16


def coords(i):
    return i >> 6, (i >> 3) & 7, (i >> 1) & 3, i & 1


def index(y, z, x, c):
    return ((y * NZ + z) * NX + x) * NC + c


def permute(value, move):
    pairs = []
    for i in range(NY * NZ * NX * NC):
        to = move(*coords(i))
        if to is not None:
            pairs.append((i, index(*to)))
    return lax.ppermute(value, SEQ, pairs)


def swap_cores(value):
    return permute(value, lambda y, z, x, c: (y, z, x, 1 - c))


def x_partner(m):
    return lambda y, z, x, c: (y, z, x ^ m, c)


def y_partner(m):
    return lambda y, z, x, c: (y ^ m, z, x, c)


def z_partner(m):
    return lambda y, z, x, c: (y, z ^ m, x, c)


def last_near(y, z, x, c):
    return (y, z, x, 1 - c) if z >> 2 == c else (y, z ^ 6, x, c)


def last_far(y, z, x, c):
    return None if z >> 2 == c else (y, z ^ 6, x, 1 - c)


def rows_dot(a, b):
    return lax.dot_general(a, b, (((0,), (0,)), ((), ())), preferred_element_type=F32)


def lanes_dot(a, b):
    return lax.dot_general(a, b, (((1,), (1,)), ((), ())), preferred_element_type=F32)


def dot(a, b):
    return jnp.dot(a, b, preferred_element_type=F32)


def head(array, h):
    return array[h * HEAD : (h + 1) * HEAD]


PACKED = (144, 128)


def pack(pair, ref):
    ref[0:96, 0:96] = pair[0]
    ref[0:96, 96:128] = pair[1][:, 0:32]
    ref[96:144, 0:64] = pair[1][0:48, 32:96]
    ref[96:144, 64:128] = pair[1][48:96, 32:96]


def unpack(array):
    rest = jnp.concatenate([array[96:144, 0:64], array[96:144, 64:128]], axis=0)
    return array[0:96, 0:96], jnp.concatenate([array[0:96, 96:128], rest], axis=1)


def states_kernel(*refs):
    sources, (keep, send, wide), held, arrived = refs[:4], refs[4:7], refs[7:11], refs[11]
    copies = [pltpu.make_async_copy(a, b, arrived.at[n]) for n, (a, b) in enumerate(zip(sources, held))]
    for copy in copies:
        copy.start()
    for copy in copies:
        copy.wait()
    q, k, v, g = held
    first = lax.axis_index(SEQ) & 1 == 0
    key_state = [lanes_dot(head(k[...], h), head(v[...], h)) for h in range(2)]
    query_state = [lanes_dot(head(q[...], h), head(g[...], h)) for h in range(2)]
    pack([jnp.where(first, a, b) for a, b in zip(key_state, query_state)], keep)
    pack([jnp.where(first, b, a) for a, b in zip(key_state, query_state)], send)
    for n, ref in enumerate(held):
        wide[n] = ref[...].astype(F32)


def halves_kernel(place, x, mine, wide, held, widened, arrived, left):
    lanes = held.shape[3]
    into, out = [], []
    for n, core in enumerate((1 - place[0], place[0])):
        for y in range(NY):
            at = pl.multiple_of((2 * y + core) * lanes, 128)
            to = wide.at[y] if n == 0 else mine.at[y]
            source = widened.at[y] if n == 0 else held.at[1, y]
            into.append(pltpu.make_async_copy(x.at[:, pl.ds(at, lanes)], held.at[n, y], arrived.at[n, y]))
            out.append(pltpu.make_async_copy(source, to, left.at[n, y]))
    for copy in into:
        copy.start()
    for n in range(2 * NY):
        into[n].wait()
        if n < NY:
            widened[n] = held[0, n].astype(F32)
        out[n].start()
    for copy in out:
        copy.wait()


def local_kernel(place, own, other, *outs):
    first = place[0] == 0
    mine, theirs = ([ref[n].astype(BF16) for n in range(4)] for ref in (own, other))
    early = [jnp.where(first, a, b) for a, b in zip(mine, theirs)]
    late = [jnp.where(first, b, a) for a, b in zip(mine, theirs)]
    length = mine[0].shape[1]
    s = lax.broadcasted_iota(jnp.int32, (length, length), 0)
    t = lax.broadcasted_iota(jnp.int32, (length, length), 1)
    causal = s <= t
    for core, (qt, kt, vt, gt) in enumerate((early, late)):
        for out, a in zip(outs, (gt, vt, kt)):
            out[core, WIDTH : 2 * WIDTH, :] = a
        for h in range(2):
            qh, kh, vh, gh = (head(a, h) for a in (qt, kt, vt, gt))
            vg = jnp.where(causal, rows_dot(vh, gh), 0.0).astype(BF16)
            kq = jnp.where(causal, rows_dot(kh, qh), 0.0).astype(BF16)
            dq = dot(kh, vg)
            dk = lanes_dot(qh, vg)
            dv = lanes_dot(gh, kq)
            if core == 0:
                state = lanes_dot(head(late[0], h), head(late[3], h)).astype(BF16)
                dk = dk + dot(state, vh)
                dv = dv + rows_dot(state, kh)
            else:
                state = lanes_dot(head(early[1], h), head(early[2], h)).astype(BF16)
                dq = dq + dot(state, gh)
            for out, a in zip(outs, (dq, dk, dv)):
                out[core, h * HEAD : (h + 1) * HEAD, :] = a.astype(BF16)


def terms_kernel(place, x, wide, d, inner, outer, held):
    c, pz = place[0], place[3]
    contract = (((0,), (1,)), ((), ()))
    for y in range(NY):
        total = lax.dot_general(x[y], d[c], contract, preferred_element_type=F32)
        theirs = wide[y].astype(BF16)
        total = total + lax.dot_general(theirs, d[1 - c], contract, preferred_element_type=F32)
        held[y] = total.reshape(held.shape[1:])
        for part in range(2):
            pair = [pz ^ (2 * part + k) for k in range(2)]
            for x_to in range(NX):
                for side in range(2):
                    rows = slice(x_to * 24 + side * 12, x_to * 24 + side * 12 + 12)
                    value = jnp.concatenate([held[y, z, rows, :] for z in pair], axis=0)
                    inner[part, side, x_to, y] = value[:, :WIDTH]
                    outer[part, side, x_to, y] = value[:, WIDTH:]


COLUMNS = (((0, 0), (0, 1), (1, 0)), ((1, 1), (2, 0), (2, 1)))
ORDERS = ((0, 1, 3, 2), (0, 3, 1, 2))


def join_kernel(factor, half, place, own, other, *refs):
    inner, outer, outs = refs[0:3], refs[3:6], refs[6:]
    first, px, py = place[0] == 0, place[1], place[2]

    def by_head(state):
        one, two = unpack(state)
        none = jnp.zeros_like(one)
        rows = [jnp.concatenate(pair, axis=1) for pair in ((one, none), (none, two))]
        return jnp.concatenate(rows, axis=0).astype(BF16)

    before = by_head(jnp.where(first, own[...], other[...]))
    later = by_head(jnp.where(first, other[...], own[...]))
    steps = ((before, lanes_dot), (later, lanes_dot), (later, dot))
    for part in range(2):
        for axis in range(2):
            out = outs[part * 2 + axis]
            for sa in range(2):
                a = ORDERS[part][2 * half + sa]
                at = [(px ^ a, py ^ b) if axis == 0 else (px ^ b, py ^ a) for b in range(4)]
                pieces = []
                for w, side in COLUMNS[axis]:
                    state, multiply = steps[w]
                    term = jnp.concatenate([outer[w][part, side, i, j] for i, j in at], axis=0)
                    add = jnp.concatenate([inner[w][part, side, i, j] for i, j in at], axis=0)
                    high = term.astype(BF16)
                    low = (term - high.astype(F32)).astype(BF16)
                    pieces.append(factor * (add + multiply(high, state) + multiply(low, state)))
                out[sa] = jnp.concatenate(pieces, axis=1).reshape(out.shape[1:])


VMEM = pl.BlockSpec(memory_space=pltpu.VMEM)
SMEM = pl.BlockSpec(memory_space=pltpu.SMEM)
HBM = pl.BlockSpec(memory_space=pltpu.HBM)
ANY = pl.BlockSpec(memory_space=pl.ANY)


def cost(flops, moved):
    return pl.CostEstimate(flops=flops, bytes_accessed=moved, transcendentals=0)


def limit(mib):
    return pltpu.CompilerParams(vmem_limit_bytes=mib * 2**20)


def states(*features):
    shape = jax.ShapeDtypeStruct(PACKED, F32)
    return pl.pallas_call(
        states_kernel,
        name="states",
        out_shape=(shape, shape, jax.ShapeDtypeStruct((4,) + features[0].shape, F32)),
        in_specs=[HBM] * 4,
        out_specs=(VMEM,) * 3,
        scratch_shapes=[pltpu.VMEM(a.shape, BF16) for a in features] + [pltpu.SemaphoreType.DMA((4,))],
        cost_estimate=cost(4 * 512 * 192 * 192, 10**6),
    )(*features)


def halves(place, x):
    length, features = x.shape
    shape = (NY, length, features // 8)
    return pl.pallas_call(
        halves_kernel,
        name="halves",
        out_shape=(jax.ShapeDtypeStruct(shape, BF16), jax.ShapeDtypeStruct(shape, F32)),
        in_specs=[SMEM, HBM],
        out_specs=(HBM, HBM),
        scratch_shapes=[pltpu.VMEM((2,) + shape, BF16), pltpu.VMEM(shape, F32)]
        + [pltpu.SemaphoreType.DMA((2, NY))] * 2,
        cost_estimate=cost(10**6, 5 * 10**6),
        compiler_params=limit(62),
    )(place, x)


def local_terms(place, mine, theirs):
    shape = jax.ShapeDtypeStruct((2, 2 * WIDTH, mine.shape[2]), BF16)
    return pl.pallas_call(
        local_kernel,
        name="local_terms",
        out_shape=(shape,) * 3,
        in_specs=[SMEM, VMEM, VMEM],
        out_specs=(VMEM,) * 3,
        cost_estimate=cost(40 * 512 * 512 * 96, 5 * 10**6),
        compiler_params=limit(20),
    )(place, mine, theirs)


def terms(place, x, wide, d):
    shape = jax.ShapeDtypeStruct((2, 2, NX, NY, 24, WIDTH), F32)
    return pl.pallas_call(
        terms_kernel,
        name="terms",
        out_shape=(shape, shape),
        in_specs=[SMEM] + [VMEM] * 3,
        out_specs=(VMEM, VMEM),
        scratch_shapes=[pltpu.VMEM((NY, 4, 96, 2 * WIDTH), F32)],
        cost_estimate=cost(2 * 512 * 3072 * 384, 8 * 10**6),
        compiler_params=limit(20),
    )(place, x, wide, d)


def join(half, factor, place, own, other, inner, outer):
    return pl.pallas_call(
        functools.partial(join_kernel, factor, half),
        name=f"join{half}",
        out_shape=(jax.ShapeDtypeStruct((2, 4, 24, 3 * WIDTH), F32),) * 4,
        in_specs=[SMEM] + [VMEM] * 8,
        out_specs=(VMEM,) * 4,
        cost_estimate=cost(24 * 384 * 192 * 192, 8 * 10**6),
        compiler_params=limit(20),
    )(place, own, other, *inner, *outer)


def tie(*values):
    return lax.optimization_barrier(values)


def before_chip(me, total, works):
    y, z, x, c = me
    before = jnp.zeros_like(total)
    steps = (
        (x_partner(1), x & 1),
        (x_partner(3), x >> 1),
        (z_partner(1), z & 1),
        (z_partner(2), (z >> 1) & 1),
        (z_partner(6), z >> 2),
        (y_partner(1), y & 1),
        (y_partner(3), y >> 1),
    )
    for n, (move, bit) in enumerate(steps):
        came = permute(total, move)
        if n in works:
            came, total = works[n](came, total)
        before = before + jnp.where(bit != c, came, 0.0)
        total = total + came
    return before


def scatter_sum(me, keep, send):
    y, z, x, c = me
    partners = (x_partner, y_partner)
    streams = [(part, axis) for part in range(2) for axis in range(2)]
    one = {}
    for n, (part, axis) in enumerate(streams):
        came = permute(send[n], partners[axis]((3, 1)[part]))
        one[n] = (keep[n][0] + came[0], keep[n][1] + came[1])
    ends = {}
    for n, (part, axis) in enumerate(streams):
        ends[part, axis] = one[n][0] + permute(one[n][1], partners[axis]((1, 3)[part]))
    chunk = lambda axis, r: jnp.stack([ends[part, axis][r] for part in range(2)])
    value = [chunk(axis, 0) for axis in range(2)]
    for r in (2, 1, 3):
        for axis in range(2):
            value[axis] = value[axis] + permute(chunk(axis, r), partners[1 - axis](r))
    value = jnp.concatenate(value, axis=2)
    chunk = lambda r: value[r >> 1, 12 * (r & 1) : 12 * (r & 1) + 12]
    total = chunk(0)
    for r in (3, 2, 1):
        total = total + permute(chunk(r), z_partner(r))
    order = COLUMNS[0] + COLUMNS[1]
    column = lambda n: total[:, n * WIDTH : (n + 1) * WIDTH]
    sides = [
        jnp.concatenate([column(order.index((w, side))) for w in range(3)], axis=1) for side in range(2)
    ]
    block = lambda i: jnp.where(i == 0, *sides)
    same = z >> 2 == c
    total = jnp.where(same, block(c), 0.0)
    total = total + permute(block(jnp.where(same, 1 - c, c)), last_near)
    return total + permute(block(1 - c), last_far)


def per_device(inputs, query_proj, key_proj, value_proj, grad_out):
    length, width = query_proj.shape
    factor = 1.0 / (math.sqrt(HEAD) * length * lax.axis_size(SEQ))
    me = coords(lax.axis_index(SEQ))
    y, z, x, c = me
    block = (z & 3) ^ jnp.where(z >> 2 == c, 0, 2)
    place = jnp.stack([c, x, y, block]).astype(jnp.int32)
    mine = [a.T for a in (query_proj, key_proj, value_proj, grad_out)]
    keep, send, wide = states(*mine)
    theirs = swap_cores(wide)
    total = keep + swap_cores(send)
    made = {}

    def halves_work(came, total):
        total, x = tie(total, inputs)
        came, (made["mine"], half) = tie(came, halves(place, x))
        made["wide"] = swap_cores(half)
        return came, total

    def local_work(came, total):
        total, there = tie(total, theirs)
        came, made["local"] = tie(came, local_terms(place, wide, there))
        return came, total

    def terms_work(n):
        def work(came, total):
            total, d = tie(total, made["local"][n])
            came, made[n] = tie(came, terms(place, made["mine"], made["wide"], d))
            return came, total

        return work

    works = {0: halves_work, 3: local_work, 4: terms_work(0), 5: terms_work(1), 6: terms_work(2)}
    before = before_chip(me, total, works)
    across = swap_cores(before)
    inner, outer = zip(*(made[n] for n in range(3)))
    send = join(1, factor, place, before, across, inner, outer)
    keep = join(0, factor, place, before, across, inner, outer)
    summed = scatter_sum(me, keep, send)
    return (summed[:, :width], summed[:, width : 2 * width], summed[:, 2 * width :])


def solution(mesh):
    return jax.shard_map(
        per_device,
        mesh=mesh,
        in_specs=(P(SEQ, None),) * 5,
        out_specs=(P(SEQ, None),) * 3,
        check_vma=False,
    )
```

```python
import functools
import math

import jax
import jax.numpy as jnp
from jax import lax
from jax.experimental import pallas as pl
from jax.experimental.pallas import tpu as pltpu
from jax.sharding import PartitionSpec as P

HEAD = 96
WIDTH = 2 * HEAD
NY, NZ, NX, NC = 4, 8, 4, 2
SEQ = "seq"
F32 = jnp.float32
BF16 = jnp.bfloat16


def coords(i):
    return i >> 6, (i >> 3) & 7, (i >> 1) & 3, i & 1


def index(y, z, x, c):
    return ((y * NZ + z) * NX + x) * NC + c


def permute(value, move):
    pairs = []
    for i in range(NY * NZ * NX * NC):
        to = move(*coords(i))
        if to is not None:
            pairs.append((i, index(*to)))
    return lax.ppermute(value, SEQ, pairs)


def swap_cores(value):
    return permute(value, lambda y, z, x, c: (y, z, x, 1 - c))


def x_partner(m):
    return lambda y, z, x, c: (y, z, x ^ m, c)


def y_partner(m):
    return lambda y, z, x, c: (y ^ m, z, x, c)


def z_partner(m):
    return lambda y, z, x, c: (y, z ^ m, x, c)


def first_partner(m):
    return lambda y, z, x, c: (y, z, x ^ m, c) if c == 0 else (y ^ m, z, x, c)


def second_partner(m):
    return lambda y, z, x, c: (y ^ m, z, x, c) if c == 0 else (y, z, x ^ m, c)


def last_near(y, z, x, c):
    return (y, z, x, 1 - c) if z >> 2 == c else (y, z ^ 6, x, c)


def last_far(y, z, x, c):
    return None if z >> 2 == c else (y, z ^ 6, x, 1 - c)


def rows_dot(a, b):
    return lax.dot_general(a, b, (((0,), (0,)), ((), ())), preferred_element_type=F32)


def lanes_dot(a, b):
    return lax.dot_general(a, b, (((1,), (1,)), ((), ())), preferred_element_type=F32)


def dot(a, b):
    return jnp.dot(a, b, preferred_element_type=F32)


def head(array, h):
    return array[h * HEAD : (h + 1) * HEAD]


PACKED = (144, 128)


def pack(pair, ref):
    ref[0:96, 0:96] = pair[0]
    ref[0:96, 96:128] = pair[1][:, 0:32]
    ref[96:144, 0:64] = pair[1][0:48, 32:96]
    ref[96:144, 64:128] = pair[1][48:96, 32:96]


def unpack(array):
    rest = jnp.concatenate([array[96:144, 0:64], array[96:144, 64:128]], axis=0)
    return array[0:96, 0:96], jnp.concatenate([array[0:96, 96:128], rest], axis=1)


def states_kernel(*refs):
    sources, (keep, send, wide), held, arrived = refs[:4], refs[4:7], refs[7:11], refs[11]
    copies = [pltpu.make_async_copy(a, b, arrived.at[n]) for n, (a, b) in enumerate(zip(sources, held))]
    for copy in copies:
        copy.start()
    for copy in copies:
        copy.wait()
    q, k, v, g = held
    first = lax.axis_index(SEQ) & 1 == 0
    key_state = [lanes_dot(head(k[...], h), head(v[...], h)) for h in range(2)]
    query_state = [lanes_dot(head(q[...], h), head(g[...], h)) for h in range(2)]
    pack([jnp.where(first, a, b) for a, b in zip(key_state, query_state)], keep)
    pack([jnp.where(first, b, a) for a, b in zip(key_state, query_state)], send)
    for n, ref in enumerate(held):
        wide[n] = ref[...].astype(F32)


def halves_kernel(place, x, mine, wide, held, widened, arrived, left):
    lanes = held.shape[3]
    into, out = [], []
    for n, core in enumerate((1 - place[0], place[0])):
        for y in range(NY):
            at = pl.multiple_of((2 * y + core) * lanes, 128)
            to = wide.at[y] if n == 0 else mine.at[y]
            source = widened.at[y] if n == 0 else held.at[1, y]
            into.append(pltpu.make_async_copy(x.at[:, pl.ds(at, lanes)], held.at[n, y], arrived.at[n, y]))
            out.append(pltpu.make_async_copy(source, to, left.at[n, y]))
    for copy in into:
        copy.start()
    for n in range(2 * NY):
        into[n].wait()
        if n < NY:
            widened[n] = held[0, n].astype(F32)
        out[n].start()
    for copy in out:
        copy.wait()


def local_kernel(place, own, other, *outs):
    first = place[0] == 0
    mine, theirs = ([ref[n].astype(BF16) for n in range(4)] for ref in (own, other))
    early = [jnp.where(first, a, b) for a, b in zip(mine, theirs)]
    late = [jnp.where(first, b, a) for a, b in zip(mine, theirs)]
    length = mine[0].shape[1]
    s = lax.broadcasted_iota(jnp.int32, (length, length), 0)
    t = lax.broadcasted_iota(jnp.int32, (length, length), 1)
    causal = s <= t
    for core, (qt, kt, vt, gt) in enumerate((early, late)):
        for out, a in zip(outs, (gt, vt, kt)):
            out[core, WIDTH : 2 * WIDTH, :] = a
        for h in range(2):
            qh, kh, vh, gh = (head(a, h) for a in (qt, kt, vt, gt))
            vg = jnp.where(causal, rows_dot(vh, gh), 0.0).astype(BF16)
            kq = jnp.where(causal, rows_dot(kh, qh), 0.0).astype(BF16)
            dq = dot(kh, vg)
            dk = lanes_dot(qh, vg)
            dv = lanes_dot(gh, kq)
            if core == 0:
                state = lanes_dot(head(late[0], h), head(late[3], h)).astype(BF16)
                dk = dk + dot(state, vh)
                dv = dv + rows_dot(state, kh)
            else:
                state = lanes_dot(head(early[1], h), head(early[2], h)).astype(BF16)
                dq = dq + dot(state, gh)
            for out, a in zip(outs, (dq, dk, dv)):
                out[core, h * HEAD : (h + 1) * HEAD, :] = a.astype(BF16)


def terms_kernel(place, x, wide, d, inner, outer, held):
    c, pz = place[0], place[3]
    contract = (((0,), (1,)), ((), ()))
    for y in range(NY):
        total = lax.dot_general(x[y], d[c], contract, preferred_element_type=F32)
        theirs = wide[y].astype(BF16)
        total = total + lax.dot_general(theirs, d[1 - c], contract, preferred_element_type=F32)
        held[y] = total.reshape(held.shape[1:])
        for part in range(2):
            pair = [pz ^ (2 * part + k) for k in range(2)]
            for x_to in range(NX):
                for side in range(2):
                    rows = slice(x_to * 24 + side * 12, x_to * 24 + side * 12 + 12)
                    value = jnp.concatenate([held[y, z, rows, :] for z in pair], axis=0)
                    inner[part, side, x_to, y] = value[:, :WIDTH]
                    outer[part, side, x_to, y] = value[:, WIDTH:]


COLUMNS = tuple((w, side) for w in range(3) for side in range(2))
ORDERS = ((0, 1, 3, 2), (0, 3, 1, 2))


def join_kernel(factor, half, place, own, other, *refs):
    inner, outer, outs = refs[0:3], refs[3:6], refs[6:]
    first, px, py = place[0] == 0, place[1], place[2]

    def by_head(state):
        one, two = unpack(state)
        none = jnp.zeros_like(one)
        rows = [jnp.concatenate(pair, axis=1) for pair in ((one, none), (none, two))]
        return jnp.concatenate(rows, axis=0).astype(BF16)

    before = by_head(jnp.where(first, own[...], other[...]))
    later = by_head(jnp.where(first, other[...], own[...]))
    steps = ((before, lanes_dot), (later, lanes_dot), (later, dot))
    for part in range(2):
        out = outs[part]
        for sa in range(2):
            a = ORDERS[part][2 * half + sa]
            at = [(jnp.where(first, px ^ a, px ^ b), jnp.where(first, py ^ b, py ^ a)) for b in range(4)]
            pieces = []
            for w, side in COLUMNS:
                state, multiply = steps[w]
                term = jnp.concatenate([outer[w][part, side, i, j] for i, j in at], axis=0)
                add = jnp.concatenate([inner[w][part, side, i, j] for i, j in at], axis=0)
                high = term.astype(BF16)
                low = (term - high.astype(F32)).astype(BF16)
                pieces.append(factor * (add + multiply(high, state) + multiply(low, state)))
            out[sa] = jnp.concatenate(pieces, axis=1).reshape(out.shape[1:])


VMEM = pl.BlockSpec(memory_space=pltpu.VMEM)
SMEM = pl.BlockSpec(memory_space=pltpu.SMEM)
HBM = pl.BlockSpec(memory_space=pltpu.HBM)
ANY = pl.BlockSpec(memory_space=pl.ANY)


def cost(flops, moved):
    return pl.CostEstimate(flops=flops, bytes_accessed=moved, transcendentals=0)


def limit(mib):
    return pltpu.CompilerParams(vmem_limit_bytes=mib * 2**20)


def states(*features):
    shape = jax.ShapeDtypeStruct(PACKED, F32)
    return pl.pallas_call(
        states_kernel,
        name="states",
        out_shape=(shape, shape, jax.ShapeDtypeStruct((4,) + features[0].shape, F32)),
        in_specs=[HBM] * 4,
        out_specs=(VMEM,) * 3,
        scratch_shapes=[pltpu.VMEM(a.shape, BF16) for a in features] + [pltpu.SemaphoreType.DMA((4,))],
        cost_estimate=cost(4 * 512 * 192 * 192, 10**6),
    )(*features)


def halves(place, x):
    length, features = x.shape
    shape = (NY, length, features // 8)
    return pl.pallas_call(
        halves_kernel,
        name="halves",
        out_shape=(jax.ShapeDtypeStruct(shape, BF16), jax.ShapeDtypeStruct(shape, F32)),
        in_specs=[SMEM, HBM],
        out_specs=(HBM, HBM),
        scratch_shapes=[pltpu.VMEM((2,) + shape, BF16), pltpu.VMEM(shape, F32)]
        + [pltpu.SemaphoreType.DMA((2, NY))] * 2,
        cost_estimate=cost(10**6, 5 * 10**6),
        compiler_params=limit(62),
    )(place, x)


def local_terms(place, mine, theirs):
    shape = jax.ShapeDtypeStruct((2, 2 * WIDTH, mine.shape[2]), BF16)
    return pl.pallas_call(
        local_kernel,
        name="local_terms",
        out_shape=(shape,) * 3,
        in_specs=[SMEM, VMEM, VMEM],
        out_specs=(VMEM,) * 3,
        cost_estimate=cost(40 * 512 * 512 * 96, 5 * 10**6),
        compiler_params=limit(20),
    )(place, mine, theirs)


def terms(place, x, wide, d):
    shape = jax.ShapeDtypeStruct((2, 2, NX, NY, 24, WIDTH), F32)
    return pl.pallas_call(
        terms_kernel,
        name="terms",
        out_shape=(shape, shape),
        in_specs=[SMEM] + [VMEM] * 3,
        out_specs=(VMEM, VMEM),
        scratch_shapes=[pltpu.VMEM((NY, 4, 96, 2 * WIDTH), F32)],
        cost_estimate=cost(2 * 512 * 3072 * 384, 8 * 10**6),
        compiler_params=limit(20),
    )(place, x, wide, d)


def join(half, factor, place, own, other, inner, outer):
    return pl.pallas_call(
        functools.partial(join_kernel, factor, half),
        name=f"join{half}",
        out_shape=(jax.ShapeDtypeStruct((2, 4, 24, 6 * WIDTH), F32),) * 2,
        in_specs=[SMEM] + [VMEM] * 8,
        out_specs=(VMEM,) * 2,
        cost_estimate=cost(24 * 384 * 192 * 192, 8 * 10**6),
        compiler_params=limit(20),
    )(place, own, other, *inner, *outer)


def tie(*values):
    return lax.optimization_barrier(values)


def before_chip(me, total, works):
    y, z, x, c = me
    before = jnp.zeros_like(total)
    steps = (
        (x_partner(1), x & 1),
        (x_partner(3), x >> 1),
        (z_partner(1), z & 1),
        (z_partner(2), (z >> 1) & 1),
        (z_partner(6), z >> 2),
        (y_partner(1), y & 1),
        (y_partner(3), y >> 1),
    )
    for n, (move, bit) in enumerate(steps):
        came = permute(total, move)
        if n in works:
            came, total = works[n](came, total)
        before = before + jnp.where(bit != c, came, 0.0)
        total = total + came
    return before


def scatter_sum(me, keep, send):
    y, z, x, c = me
    one = []
    for part in range(2):
        came = permute(send[part], first_partner((3, 1)[part]))
        one.append((keep[part][0] + came[0], keep[part][1] + came[1]))
    ends = [one[part][0] + permute(one[part][1], first_partner((1, 3)[part])) for part in range(2)]
    chunk = lambda r: jnp.stack([end[r] for end in ends])
    value = chunk(0)
    for r in (2, 1, 3):
        value = value + permute(chunk(r), second_partner(r))
    chunk = lambda r: value[r >> 1, 12 * (r & 1) : 12 * (r & 1) + 12]
    total = chunk(0)
    for r in (3, 2, 1):
        total = total + permute(chunk(r), z_partner(r))
    column = lambda n: total[:, n * WIDTH : (n + 1) * WIDTH]
    sides = [
        jnp.concatenate([column(COLUMNS.index((w, side))) for w in range(3)], axis=1) for side in range(2)
    ]
    block = lambda i: jnp.where(i == 0, *sides)
    same = z >> 2 == c
    total = jnp.where(same, block(c), 0.0)
    total = total + permute(block(jnp.where(same, 1 - c, c)), last_near)
    return total + permute(block(1 - c), last_far)


def per_device(inputs, query_proj, key_proj, value_proj, grad_out):
    length, width = query_proj.shape
    factor = 1.0 / (math.sqrt(HEAD) * length * lax.axis_size(SEQ))
    me = coords(lax.axis_index(SEQ))
    y, z, x, c = me
    block = (z & 3) ^ jnp.where(z >> 2 == c, 0, 2)
    place = jnp.stack([c, x, y, block]).astype(jnp.int32)
    mine = [a.T for a in (query_proj, key_proj, value_proj, grad_out)]
    keep, send, wide = states(*mine)
    theirs = swap_cores(wide)
    total = keep + swap_cores(send)
    made = {}

    def halves_work(came, total):
        total, x = tie(total, inputs)
        came, (made["mine"], half) = tie(came, halves(place, x))
        made["wide"] = swap_cores(half)
        return came, total

    def local_work(came, total):
        total, there = tie(total, theirs)
        came, made["local"] = tie(came, local_terms(place, wide, there))
        return came, total

    def terms_work(n):
        def work(came, total):
            total, d = tie(total, made["local"][n])
            came, made[n] = tie(came, terms(place, made["mine"], made["wide"], d))
            return came, total

        return work

    works = {0: halves_work, 3: local_work, 4: terms_work(0), 5: terms_work(1), 6: terms_work(2)}
    before = before_chip(me, total, works)
    across = swap_cores(before)
    inner, outer = zip(*(made[n] for n in range(3)))
    send = join(1, factor, place, before, across, inner, outer)
    keep = join(0, factor, place, before, across, inner, outer)
    summed = scatter_sum(me, keep, send)
    return (summed[:, :width], summed[:, width : 2 * width], summed[:, 2 * width :])


def solution(mesh):
    return jax.shard_map(
        per_device,
        mesh=mesh,
        in_specs=(P(SEQ, None),) * 5,
        out_specs=(P(SEQ, None),) * 3,
        check_vma=False,
    )
```

```python
import functools
import math

import jax
import jax.numpy as jnp
from jax import lax
from jax.experimental import pallas as pl
from jax.experimental.pallas import tpu as pltpu
from jax.sharding import PartitionSpec as P

HEAD = 96
WIDTH = 2 * HEAD
NY, NZ, NX, NC = 4, 8, 4, 2
SEQ = "seq"
F32 = jnp.float32
BF16 = jnp.bfloat16


def coords(i):
    return i >> 6, (i >> 3) & 7, (i >> 1) & 3, i & 1


def index(y, z, x, c):
    return ((y * NZ + z) * NX + x) * NC + c


def permute(value, move):
    pairs = []
    for i in range(NY * NZ * NX * NC):
        to = move(*coords(i))
        if to is not None:
            pairs.append((i, index(*to)))
    return lax.ppermute(value, SEQ, pairs)


def swap_cores(value):
    return permute(value, lambda y, z, x, c: (y, z, x, 1 - c))


def x_partner(m):
    return lambda y, z, x, c: (y, z, x ^ m, c)


def y_partner(m):
    return lambda y, z, x, c: (y ^ m, z, x, c)


def z_partner(m):
    return lambda y, z, x, c: (y, z ^ m, x, c)


def first_partner(m):
    return lambda y, z, x, c: (y, z, x ^ m, c) if c == 0 else (y ^ m, z, x, c)


def second_partner(m):
    return lambda y, z, x, c: (y ^ m, z, x, c) if c == 0 else (y, z, x ^ m, c)


def last_near(y, z, x, c):
    return (y, z, x, 1 - c) if z >> 2 == c else (y, z ^ 6, x, c)


def last_far(y, z, x, c):
    return None if z >> 2 == c else (y, z ^ 6, x, 1 - c)


def rows_dot(a, b):
    return lax.dot_general(a, b, (((0,), (0,)), ((), ())), preferred_element_type=F32)


def lanes_dot(a, b):
    return lax.dot_general(a, b, (((1,), (1,)), ((), ())), preferred_element_type=F32)


def dot(a, b):
    return jnp.dot(a, b, preferred_element_type=F32)


def head(array, h):
    return array[h * HEAD : (h + 1) * HEAD]


PACKED = (144, 128)


def pack(pair, ref):
    ref[0:96, 0:96] = pair[0]
    ref[0:96, 96:128] = pair[1][:, 0:32]
    ref[96:144, 0:64] = pair[1][0:48, 32:96]
    ref[96:144, 64:128] = pair[1][48:96, 32:96]


def unpack(array):
    rest = jnp.concatenate([array[96:144, 0:64], array[96:144, 64:128]], axis=0)
    return array[0:96, 0:96], jnp.concatenate([array[0:96, 96:128], rest], axis=1)


def states_kernel(*refs):
    sources, (keep, send, wide), held, arrived = refs[:4], refs[4:7], refs[7:11], refs[11]
    copies = [pltpu.make_async_copy(a, b, arrived.at[n]) for n, (a, b) in enumerate(zip(sources, held))]
    for copy in copies:
        copy.start()
    for copy in copies:
        copy.wait()
    q, k, v, g = held
    first = lax.axis_index(SEQ) & 1 == 0
    key_state = [lanes_dot(head(k[...], h), head(v[...], h)) for h in range(2)]
    query_state = [lanes_dot(head(q[...], h), head(g[...], h)) for h in range(2)]
    pack([jnp.where(first, a, b) for a, b in zip(key_state, query_state)], keep)
    pack([jnp.where(first, b, a) for a, b in zip(key_state, query_state)], send)
    for n, ref in enumerate(held):
        wide[n] = ref[...].astype(F32)


def halves_kernel(place, x, mine, wide, held, widened, arrived, left):
    lanes = held.shape[3]
    into, out = [], []
    for n, core in enumerate((1 - place[0], place[0])):
        for y in range(NY):
            at = pl.multiple_of((2 * y + core) * lanes, 128)
            to = wide.at[y] if n == 0 else mine.at[y]
            source = widened.at[y] if n == 0 else held.at[1, y]
            into.append(pltpu.make_async_copy(x.at[:, pl.ds(at, lanes)], held.at[n, y], arrived.at[n, y]))
            out.append(pltpu.make_async_copy(source, to, left.at[n, y]))
    for copy in into:
        copy.start()
    for n in range(2 * NY):
        into[n].wait()
        if n < NY:
            widened[n] = held[0, n].astype(F32)
        out[n].start()
    for copy in out:
        copy.wait()


def local_kernel(place, own, other, *outs):
    first = place[0] == 0
    mine, theirs = ([ref[n].astype(BF16) for n in range(4)] for ref in (own, other))
    early = [jnp.where(first, a, b) for a, b in zip(mine, theirs)]
    late = [jnp.where(first, b, a) for a, b in zip(mine, theirs)]
    length = mine[0].shape[1]
    s = lax.broadcasted_iota(jnp.int32, (length, length), 0)
    t = lax.broadcasted_iota(jnp.int32, (length, length), 1)
    causal = s <= t
    for core, (qt, kt, vt, gt) in enumerate((early, late)):
        for out, a in zip(outs, (gt, vt, kt)):
            out[core, WIDTH : 2 * WIDTH, :] = a
        for h in range(2):
            qh, kh, vh, gh = (head(a, h) for a in (qt, kt, vt, gt))
            vg = jnp.where(causal, rows_dot(vh, gh), 0.0).astype(BF16)
            kq = jnp.where(causal, rows_dot(kh, qh), 0.0).astype(BF16)
            dq = dot(kh, vg)
            dk = lanes_dot(qh, vg)
            dv = lanes_dot(gh, kq)
            if core == 0:
                state = lanes_dot(head(late[0], h), head(late[3], h)).astype(BF16)
                dk = dk + dot(state, vh)
                dv = dv + rows_dot(state, kh)
            else:
                state = lanes_dot(head(early[1], h), head(early[2], h)).astype(BF16)
                dq = dq + dot(state, gh)
            for out, a in zip(outs, (dq, dk, dv)):
                out[core, h * HEAD : (h + 1) * HEAD, :] = a.astype(BF16)


def terms_kernel(place, x, wide, d, inner, outer, held):
    c, pz = place[0], place[3]
    contract = (((0,), (1,)), ((), ()))
    for y in range(NY):
        total = lax.dot_general(x[y], d[c], contract, preferred_element_type=F32)
        theirs = wide[y].astype(BF16)
        total = total + lax.dot_general(theirs, d[1 - c], contract, preferred_element_type=F32)
        held[y] = total.reshape(held.shape[1:])
        for part in range(2):
            pair = [pz ^ (2 * part + k) for k in range(2)]
            for x_to in range(NX):
                for side in range(2):
                    rows = slice(x_to * 24 + side * 12, x_to * 24 + side * 12 + 12)
                    value = jnp.concatenate([held[y, z, rows, :] for z in pair], axis=0)
                    inner[part, side, x_to, y] = value[:, :WIDTH]
                    outer[part, side, x_to, y] = value[:, WIDTH:]


COLUMNS = tuple((w, side) for w in range(3) for side in range(2))
ORDERS = ((0, 1, 3, 2), (0, 3, 1, 2))


def join_kernel(factor, half, place, own, other, *refs):
    inner, outer, outs = refs[0:3], refs[3:6], refs[6:]
    first, px, py = place[0] == 0, place[1], place[2]

    def by_head(state):
        one, two = unpack(state)
        none = jnp.zeros_like(one)
        rows = [jnp.concatenate(pair, axis=1) for pair in ((one, none), (none, two))]
        return jnp.concatenate(rows, axis=0).astype(BF16)

    before = by_head(jnp.where(first, own[...], other[...]))
    later = by_head(jnp.where(first, other[...], own[...]))
    steps = ((before, lanes_dot), (later, lanes_dot), (later, dot))
    for part in range(2):
        out = outs[part]
        for sa in range(2):
            a = ORDERS[part][2 * half + sa]
            at = [(jnp.where(first, px ^ a, px ^ b), jnp.where(first, py ^ b, py ^ a)) for b in range(4)]
            pieces = []
            for w, side in COLUMNS:
                state, multiply = steps[w]
                term = jnp.concatenate([outer[w][part, side, i, j] for i, j in at], axis=0)
                add = jnp.concatenate([inner[w][part, side, i, j] for i, j in at], axis=0)
                high = term.astype(BF16)
                low = (term - high.astype(F32)).astype(BF16)
                pieces.append(factor * (add + multiply(high, state) + multiply(low, state)))
            out[sa] = jnp.concatenate(pieces, axis=1).reshape(out.shape[1:])


VMEM = pl.BlockSpec(memory_space=pltpu.VMEM)
SMEM = pl.BlockSpec(memory_space=pltpu.SMEM)
HBM = pl.BlockSpec(memory_space=pltpu.HBM)
ANY = pl.BlockSpec(memory_space=pl.ANY)


def cost(flops, moved):
    return pl.CostEstimate(flops=flops, bytes_accessed=moved, transcendentals=0)


def limit(mib):
    return pltpu.CompilerParams(vmem_limit_bytes=mib * 2**20)


def states(*features):
    shape = jax.ShapeDtypeStruct(PACKED, F32)
    return pl.pallas_call(
        states_kernel,
        name="states",
        out_shape=(shape, shape, jax.ShapeDtypeStruct((4,) + features[0].shape, F32)),
        in_specs=[HBM] * 4,
        out_specs=(VMEM,) * 3,
        scratch_shapes=[pltpu.VMEM(a.shape, BF16) for a in features] + [pltpu.SemaphoreType.DMA((4,))],
        cost_estimate=cost(4 * 512 * 192 * 192, 10**6),
    )(*features)


def halves(place, x):
    length, features = x.shape
    shape = (NY, length, features // 8)
    return pl.pallas_call(
        halves_kernel,
        name="halves",
        out_shape=(jax.ShapeDtypeStruct(shape, BF16), jax.ShapeDtypeStruct(shape, F32)),
        in_specs=[SMEM, HBM],
        out_specs=(HBM, HBM),
        scratch_shapes=[pltpu.VMEM((2,) + shape, BF16), pltpu.VMEM(shape, F32)]
        + [pltpu.SemaphoreType.DMA((2, NY))] * 2,
        cost_estimate=cost(10**6, 5 * 10**6),
        compiler_params=limit(16),
    )(place, x)


def local_terms(place, mine, theirs):
    shape = jax.ShapeDtypeStruct((2, 2 * WIDTH, mine.shape[2]), BF16)
    return pl.pallas_call(
        local_kernel,
        name="local_terms",
        out_shape=(shape,) * 3,
        in_specs=[SMEM, VMEM, VMEM],
        out_specs=(VMEM,) * 3,
        cost_estimate=cost(40 * 512 * 512 * 96, 5 * 10**6),
        compiler_params=limit(20),
    )(place, mine, theirs)


def terms(place, x, wide, d):
    shape = jax.ShapeDtypeStruct((2, 2, NX, NY, 24, WIDTH), F32)
    return pl.pallas_call(
        terms_kernel,
        name="terms",
        out_shape=(shape, shape),
        in_specs=[SMEM] + [VMEM] * 3,
        out_specs=(VMEM, VMEM),
        scratch_shapes=[pltpu.VMEM((NY, 4, 96, 2 * WIDTH), F32)],
        cost_estimate=cost(2 * 512 * 3072 * 384, 8 * 10**6),
        compiler_params=limit(20),
    )(place, x, wide, d)


def join(half, factor, place, own, other, inner, outer):
    return pl.pallas_call(
        functools.partial(join_kernel, factor, half),
        name=f"join{half}",
        out_shape=(jax.ShapeDtypeStruct((2, 4, 24, 6 * WIDTH), F32),) * 2,
        in_specs=[SMEM] + [VMEM] * 8,
        out_specs=(VMEM,) * 2,
        cost_estimate=cost(24 * 384 * 192 * 192, 8 * 10**6),
        compiler_params=limit(20),
    )(place, own, other, *inner, *outer)


def tie(*values):
    return lax.optimization_barrier(values)


def before_chip(me, total, works):
    y, z, x, c = me
    before = jnp.zeros_like(total)
    steps = (
        (x_partner, x, ((1, 1), (3, 3), (2, 2))),
        (z_partner, z & 3, ((1, 1), (2, 2), (3, 3))),
        (z_partner, z >> 2, ((6, 1),)),
        (y_partner, y, ((1, 1), (3, 3), (2, 2))),
    )
    for n, (partner, place, others) in enumerate(steps):
        came = [permute(total, partner(move)) for move, _ in others]
        for work in works[n]:
            came, total = work(came, total)
        for a, (_, other) in zip(came, others):
            earlier = (place ^ other < place) == (c == 0)
            before = before + jnp.where(earlier, a, 0.0)
            total = total + a
    return before


def scatter_sum(me, keep, send):
    y, z, x, c = me
    one = []
    for part in range(2):
        came = permute(send[part], first_partner((3, 1)[part]))
        one.append((keep[part][0] + came[0], keep[part][1] + came[1]))
    ends = [one[part][0] + permute(one[part][1], first_partner((1, 3)[part])) for part in range(2)]
    chunk = lambda r: jnp.stack([end[r] for end in ends])
    value = chunk(0)
    for r in (2, 1, 3):
        value = value + permute(chunk(r), second_partner(r))
    chunk = lambda r: value[r >> 1, 12 * (r & 1) : 12 * (r & 1) + 12]
    total = chunk(0)
    for r in (3, 2, 1):
        total = total + permute(chunk(r), z_partner(r))
    column = lambda n: total[:, n * WIDTH : (n + 1) * WIDTH]
    sides = [
        jnp.concatenate([column(COLUMNS.index((w, side))) for w in range(3)], axis=1) for side in range(2)
    ]
    block = lambda i: jnp.where(i == 0, *sides)
    same = z >> 2 == c
    total = jnp.where(same, block(c), 0.0)
    total = total + permute(block(jnp.where(same, 1 - c, c)), last_near)
    return total + permute(block(1 - c), last_far)


def per_device(inputs, query_proj, key_proj, value_proj, grad_out):
    length, width = query_proj.shape
    factor = 1.0 / (math.sqrt(HEAD) * length * lax.axis_size(SEQ))
    me = coords(lax.axis_index(SEQ))
    y, z, x, c = me
    block = (z & 3) ^ jnp.where(z >> 2 == c, 0, 2)
    place = jnp.stack([c, x, y, block]).astype(jnp.int32)
    mine = [a.T for a in (query_proj, key_proj, value_proj, grad_out)]
    keep, send, wide = states(*mine)
    came, sent = tie(swap_cores(send), wide)
    theirs = swap_cores(sent)
    total = keep + came
    made = {}

    def halves_work(came, total):
        total, x, made["theirs"] = tie(total, inputs, theirs)
        came, (made["mine"], half) = tie(came, halves(place, x))
        made["wide"] = swap_cores(half)
        return came, total

    def local_work(came, total):
        total, there = tie(total, made["theirs"])
        came, made["local"] = tie(came, local_terms(place, wide, there))
        return came, total

    def terms_work(n):
        def work(came, total):
            total, d = tie(total, made["local"][n])
            came, made[n] = tie(came, terms(place, made["mine"], made["wide"], d))
            return came, total

        return work

    works = ((halves_work,), (local_work,), (terms_work(0),), (terms_work(1), terms_work(2)))
    before = before_chip(me, total, works)
    across = swap_cores(before)
    inner, outer = zip(*(made[n] for n in range(3)))
    send = join(1, factor, place, before, across, inner, outer)
    keep = join(0, factor, place, before, across, inner, outer)
    summed = scatter_sum(me, keep, send)
    return (summed[:, :width], summed[:, width : 2 * width], summed[:, 2 * width :])


def solution(mesh):
    return jax.shard_map(
        per_device,
        mesh=mesh,
        in_specs=(P(SEQ, None),) * 5,
        out_specs=(P(SEQ, None),) * 3,
        check_vma=False,
    )
```

```python
import functools
import math

import jax
import jax.numpy as jnp
from jax import lax
from jax.experimental import pallas as pl
from jax.experimental.pallas import tpu as pltpu
from jax.sharding import PartitionSpec as P

HEAD = 96
WIDTH = 2 * HEAD
NY, NZ, NX, NC = 4, 8, 4, 2
SEQ = "seq"
F32 = jnp.float32
BF16 = jnp.bfloat16


def coords(i):
    return i >> 6, (i >> 3) & 7, (i >> 1) & 3, i & 1


def index(y, z, x, c):
    return ((y * NZ + z) * NX + x) * NC + c


def permute(value, move):
    pairs = []
    for i in range(NY * NZ * NX * NC):
        to = move(*coords(i))
        if to is not None:
            pairs.append((i, index(*to)))
    return lax.ppermute(value, SEQ, pairs)


def swap_cores(value):
    return permute(value, lambda y, z, x, c: (y, z, x, 1 - c))


def x_partner(m):
    return lambda y, z, x, c: (y, z, x ^ m, c)


def y_partner(m):
    return lambda y, z, x, c: (y ^ m, z, x, c)


def z_partner(m):
    return lambda y, z, x, c: (y, z ^ m, x, c)


def first_partner(m):
    return lambda y, z, x, c: (y, z, x ^ m, c) if c == 0 else (y ^ m, z, x, c)


def second_partner(m):
    return lambda y, z, x, c: (y ^ m, z, x, c) if c == 0 else (y, z, x ^ m, c)


def last_near(y, z, x, c):
    return (y, z, x, 1 - c) if z >> 2 == c else (y, z ^ 6, x, c)


def last_far(y, z, x, c):
    return None if z >> 2 == c else (y, z ^ 6, x, 1 - c)


def rows_dot(a, b):
    return lax.dot_general(a, b, (((0,), (0,)), ((), ())), preferred_element_type=F32)


def lanes_dot(a, b):
    return lax.dot_general(a, b, (((1,), (1,)), ((), ())), preferred_element_type=F32)


def dot(a, b):
    return jnp.dot(a, b, preferred_element_type=F32)


def head(array, h):
    return array[h * HEAD : (h + 1) * HEAD]


PACKED = (144, 128)


def pack(pair, ref):
    ref[0:96, 0:96] = pair[0]
    ref[0:96, 96:128] = pair[1][:, 0:32]
    ref[96:144, 0:64] = pair[1][0:48, 32:96]
    ref[96:144, 64:128] = pair[1][48:96, 32:96]


def unpack(array):
    rest = jnp.concatenate([array[96:144, 0:64], array[96:144, 64:128]], axis=0)
    return array[0:96, 0:96], jnp.concatenate([array[0:96, 96:128], rest], axis=1)


def states_kernel(*refs):
    sources, (keep, send, wide), held, arrived = refs[:4], refs[4:7], refs[7:11], refs[11]
    copies = [pltpu.make_async_copy(a, b, arrived.at[n]) for n, (a, b) in enumerate(zip(sources, held))]
    for copy in copies:
        copy.start()
    for copy in copies:
        copy.wait()
    q, k, v, g = held
    first = lax.axis_index(SEQ) & 1 == 0
    key_state = [lanes_dot(head(k[...], h), head(v[...], h)) for h in range(2)]
    query_state = [lanes_dot(head(q[...], h), head(g[...], h)) for h in range(2)]
    pack([jnp.where(first, a, b) for a, b in zip(key_state, query_state)], keep)
    pack([jnp.where(first, b, a) for a, b in zip(key_state, query_state)], send)
    for n, ref in enumerate(held):
        wide[n] = ref[...].astype(F32)


def halves_kernel(place, x, mine, wide, held, widened, arrived, left):
    lanes = held.shape[3]
    into, out = [], []
    for n, core in enumerate((1 - place[0], place[0])):
        for y in range(NY):
            at = pl.multiple_of((2 * y + core) * lanes, 128)
            to = wide.at[y] if n == 0 else mine.at[y]
            source = widened.at[y] if n == 0 else held.at[1, y]
            into.append(pltpu.make_async_copy(x.at[:, pl.ds(at, lanes)], held.at[n, y], arrived.at[n, y]))
            out.append(pltpu.make_async_copy(source, to, left.at[n, y]))
    for copy in into:
        copy.start()
    for n in range(2 * NY):
        into[n].wait()
        if n < NY:
            widened[n] = held[0, n].astype(F32)
        out[n].start()
    for copy in out:
        copy.wait()


def local_kernel(place, own, other, *outs):
    first = place[0] == 0
    mine, theirs = ([ref[n].astype(BF16) for n in range(4)] for ref in (own, other))
    early = [jnp.where(first, a, b) for a, b in zip(mine, theirs)]
    late = [jnp.where(first, b, a) for a, b in zip(mine, theirs)]
    length = mine[0].shape[1]
    s = lax.broadcasted_iota(jnp.int32, (length, length), 0)
    t = lax.broadcasted_iota(jnp.int32, (length, length), 1)
    causal = s <= t
    for core, (qt, kt, vt, gt) in enumerate((early, late)):
        for out, a in zip(outs, (gt, vt, kt)):
            out[core, WIDTH : 2 * WIDTH, :] = a
        for h in range(2):
            qh, kh, vh, gh = (head(a, h) for a in (qt, kt, vt, gt))
            vg = jnp.where(causal, rows_dot(vh, gh), 0.0).astype(BF16)
            kq = jnp.where(causal, rows_dot(kh, qh), 0.0).astype(BF16)
            dq = dot(kh, vg)
            dk = lanes_dot(qh, vg)
            dv = lanes_dot(gh, kq)
            if core == 0:
                state = lanes_dot(head(late[0], h), head(late[3], h)).astype(BF16)
                dk = dk + dot(state, vh)
                dv = dv + rows_dot(state, kh)
            else:
                state = lanes_dot(head(early[1], h), head(early[2], h)).astype(BF16)
                dq = dq + dot(state, gh)
            for out, a in zip(outs, (dq, dk, dv)):
                out[core, h * HEAD : (h + 1) * HEAD, :] = a.astype(BF16)


def terms_kernel(place, x, wide, d, inner, outer, held):
    c, pz = place[0], place[3]
    contract = (((0,), (1,)), ((), ()))
    for y in range(NY):
        total = lax.dot_general(x[y], d[c], contract, preferred_element_type=F32)
        theirs = wide[y].astype(BF16)
        total = total + lax.dot_general(theirs, d[1 - c], contract, preferred_element_type=F32)
        held[y] = total.reshape(held.shape[1:])
        for part in range(2):
            pair = [pz ^ (2 * part + k) for k in range(2)]
            for x_to in range(NX):
                for side in range(2):
                    rows = slice(x_to * 24 + side * 12, x_to * 24 + side * 12 + 12)
                    value = jnp.concatenate([held[y, z, rows, :] for z in pair], axis=0)
                    inner[part, side, x_to, y] = value[:, :WIDTH]
                    outer[part, side, x_to, y] = value[:, WIDTH:]


COLUMNS = tuple((w, side) for w in range(3) for side in range(2))
ORDERS = ((0, 1, 3, 2), (0, 3, 1, 2))


def join_kernel(factor, half, place, own, other, *refs):
    inner, outer, outs = refs[0:3], refs[3:6], refs[6:]
    first, px, py = place[0] == 0, place[1], place[2]

    def by_head(state):
        one, two = unpack(state)
        none = jnp.zeros_like(one)
        rows = [jnp.concatenate(pair, axis=1) for pair in ((one, none), (none, two))]
        return jnp.concatenate(rows, axis=0).astype(BF16)

    before = by_head(jnp.where(first, own[...], other[...]))
    later = by_head(jnp.where(first, other[...], own[...]))
    steps = ((before, lanes_dot), (later, lanes_dot), (later, dot))
    for part in range(2):
        blocks = []
        for side in range(2):
            for sa in range(2):
                a = ORDERS[part][2 * half + sa]
                for b in range(4):
                    at = (jnp.where(first, px ^ a, px ^ b), jnp.where(first, py ^ b, py ^ a))
                    blocks.append((side,) + at)
        pieces = []
        for w, (state, multiply) in enumerate(steps):
            term = jnp.concatenate([outer[w][(part,) + at] for at in blocks], axis=0)
            add = jnp.concatenate([inner[w][(part,) + at] for at in blocks], axis=0)
            rows = term.shape[0]
            high = term.astype(BF16)
            low = (term - high.astype(F32)).astype(BF16)
            both = multiply(jnp.concatenate([high, low], axis=0), state)
            total = factor * (add + both[:rows] + both[rows:])
            pieces += [total[: rows // 2], total[rows // 2 :]]
        outs[part][...] = jnp.concatenate(pieces, axis=1).reshape(outs[part].shape)


VMEM = pl.BlockSpec(memory_space=pltpu.VMEM)
SMEM = pl.BlockSpec(memory_space=pltpu.SMEM)
HBM = pl.BlockSpec(memory_space=pltpu.HBM)
ANY = pl.BlockSpec(memory_space=pl.ANY)


def cost(flops, moved):
    return pl.CostEstimate(flops=flops, bytes_accessed=moved, transcendentals=0)


def limit(mib):
    return pltpu.CompilerParams(vmem_limit_bytes=mib * 2**20)


def states(*features):
    shape = jax.ShapeDtypeStruct(PACKED, F32)
    return pl.pallas_call(
        states_kernel,
        name="states",
        out_shape=(shape, shape, jax.ShapeDtypeStruct((4,) + features[0].shape, F32)),
        in_specs=[HBM] * 4,
        out_specs=(VMEM,) * 3,
        scratch_shapes=[pltpu.VMEM(a.shape, BF16) for a in features] + [pltpu.SemaphoreType.DMA((4,))],
        cost_estimate=cost(4 * 512 * 192 * 192, 10**6),
    )(*features)


def halves(place, x):
    length, features = x.shape
    shape = (NY, length, features // 8)
    return pl.pallas_call(
        halves_kernel,
        name="halves",
        out_shape=(jax.ShapeDtypeStruct(shape, BF16), jax.ShapeDtypeStruct(shape, F32)),
        in_specs=[SMEM, HBM],
        out_specs=(HBM, HBM),
        scratch_shapes=[pltpu.VMEM((2,) + shape, BF16), pltpu.VMEM(shape, F32)]
        + [pltpu.SemaphoreType.DMA((2, NY))] * 2,
        cost_estimate=cost(10**6, 5 * 10**6),
        compiler_params=limit(16),
    )(place, x)


def local_terms(place, mine, theirs):
    shape = jax.ShapeDtypeStruct((2, 2 * WIDTH, mine.shape[2]), BF16)
    return pl.pallas_call(
        local_kernel,
        name="local_terms",
        out_shape=(shape,) * 3,
        in_specs=[SMEM, VMEM, VMEM],
        out_specs=(VMEM,) * 3,
        cost_estimate=cost(40 * 512 * 512 * 96, 5 * 10**6),
        compiler_params=limit(20),
    )(place, mine, theirs)


def terms(place, x, wide, d):
    shape = jax.ShapeDtypeStruct((2, 2, NX, NY, 24, WIDTH), F32)
    return pl.pallas_call(
        terms_kernel,
        name="terms",
        out_shape=(shape, shape),
        in_specs=[SMEM] + [VMEM] * 3,
        out_specs=(VMEM, VMEM),
        scratch_shapes=[pltpu.VMEM((NY, 4, 96, 2 * WIDTH), F32)],
        cost_estimate=cost(2 * 512 * 3072 * 384, 8 * 10**6),
        compiler_params=limit(20),
    )(place, x, wide, d)


def join(half, factor, place, own, other, inner, outer):
    return pl.pallas_call(
        functools.partial(join_kernel, factor, half),
        name=f"join{half}",
        out_shape=(jax.ShapeDtypeStruct((2, 4, 24, 6 * WIDTH), F32),) * 2,
        in_specs=[SMEM] + [VMEM] * 8,
        out_specs=(VMEM,) * 2,
        cost_estimate=cost(24 * 384 * 192 * 192, 8 * 10**6),
        compiler_params=limit(20),
    )(place, own, other, *inner, *outer)


def tie(*values):
    return lax.optimization_barrier(values)


def before_chip(me, total, works):
    y, z, x, c = me
    before = jnp.zeros_like(total)
    steps = (
        (x_partner, x, ((1, 1), (3, 3), (2, 2))),
        (z_partner, z & 3, ((1, 1), (2, 2), (3, 3))),
        (z_partner, z >> 2, ((6, 1),)),
        (y_partner, y, ((1, 1), (3, 3), (2, 2))),
    )
    for n, (partner, place, others) in enumerate(steps):
        came = [permute(total, partner(move)) for move, _ in others]
        for work in works[n]:
            came, total = work(came, total)
        for a, (_, other) in zip(came, others):
            earlier = (place ^ other < place) == (c == 0)
            before = before + jnp.where(earlier, a, 0.0)
            total = total + a
    return before


def scatter_sum(me, keep, send):
    y, z, x, c = me
    one = []
    for part in range(2):
        came = permute(send[part], first_partner((3, 1)[part]))
        one.append((keep[part][0] + came[0], keep[part][1] + came[1]))
    ends = [one[part][0] + permute(one[part][1], first_partner((1, 3)[part])) for part in range(2)]
    chunk = lambda r: jnp.stack([end[r] for end in ends])
    value = chunk(0)
    for r in (2, 1, 3):
        value = value + permute(chunk(r), second_partner(r))
    chunk = lambda r: value[r >> 1, 12 * (r & 1) : 12 * (r & 1) + 12]
    total = chunk(0)
    for r in (3, 2, 1):
        total = total + permute(chunk(r), z_partner(r))
    column = lambda n: total[:, n * WIDTH : (n + 1) * WIDTH]
    sides = [
        jnp.concatenate([column(COLUMNS.index((w, side))) for w in range(3)], axis=1) for side in range(2)
    ]
    block = lambda i: jnp.where(i == 0, *sides)
    same = z >> 2 == c
    total = jnp.where(same, block(c), 0.0)
    total = total + permute(block(jnp.where(same, 1 - c, c)), last_near)
    return total + permute(block(1 - c), last_far)


def per_device(inputs, query_proj, key_proj, value_proj, grad_out):
    length, width = query_proj.shape
    factor = 1.0 / (math.sqrt(HEAD) * length * lax.axis_size(SEQ))
    me = coords(lax.axis_index(SEQ))
    y, z, x, c = me
    block = (z & 3) ^ jnp.where(z >> 2 == c, 0, 2)
    place = jnp.stack([c, x, y, block]).astype(jnp.int32)
    mine = [a.T for a in (query_proj, key_proj, value_proj, grad_out)]
    keep, send, wide = states(*mine)
    came, sent = tie(swap_cores(send), wide)
    theirs = swap_cores(sent)
    total = keep + came
    made = {}

    def halves_work(came, total):
        total, x, made["theirs"] = tie(total, inputs, theirs)
        came, (made["mine"], half) = tie(came, halves(place, x))
        made["wide"] = swap_cores(half)
        return came, total

    def local_work(came, total):
        total, there = tie(total, made["theirs"])
        came, made["local"] = tie(came, local_terms(place, wide, there))
        return came, total

    def terms_work(n):
        def work(came, total):
            total, d = tie(total, made["local"][n])
            came, made[n] = tie(came, terms(place, made["mine"], made["wide"], d))
            return came, total

        return work

    works = ((halves_work,), (local_work,), (terms_work(0),), (terms_work(1), terms_work(2)))
    before = before_chip(me, total, works)
    across = swap_cores(before)
    inner, outer = zip(*(made[n] for n in range(3)))
    send = join(1, factor, place, before, across, inner, outer)
    keep = join(0, factor, place, before, across, inner, outer)
    summed = scatter_sum(me, keep, send)
    return (summed[:, :width], summed[:, width : 2 * width], summed[:, 2 * width :])


def solution(mesh):
    return jax.shard_map(
        per_device,
        mesh=mesh,
        in_specs=(P(SEQ, None),) * 5,
        out_specs=(P(SEQ, None),) * 3,
        check_vma=False,
    )
```
